128 devices in a mesh: gx: 16 (over x, y), gy: 8 (over z, core).
Axes of the slice: x: 4, y: 4, z: 4, core: 2. Of those that a mesh axis runs over, the one named last changes fastest.
Arguments:
- rhs_loads: float32 [3, 128, 256, 768], P(None, 'gx', 'gy'), may hold values from -16 to 16
- flags: int32 [16, 32, 96], P('gx', 'gy'), may hold values from 0 to 1
- fixed: int32 [128, 256], P('gx', 'gy'), may hold values from 0 to 1, as said below
Outputs:
- adjoint: float32 [3, 128, 256, 768], P(None, 'gx', 'gy')
- residual: float32 [3, 128, 256, 768], P(None, 'gx', 'gy')
The draws below stay inside these ranges and needn't reach their ends.
Inputs may be any that keep to these rules, and one draw needn't show every extreme that they name: `fixed`: every copy of a shared node holds the same value.
All inputs are finite; a program needn't handle non-finite values.
Results may differ from the reference program's by a relative error of at most 0.0027.
Values sent between devices are 32-bit elements; how exact they have to be, the bound alone decides.
No kernel may reach another device: no remote copies, remote signals or barrier semaphores. Data moves between devices by JAX's collectives and lax.ppermute only.
A program may use at most 64 MiB of HBM per device.

```python
import jax
import jax.numpy as jnp
import numpy as np
from jax import lax

ORDER = 7
EZ = 96
ITERS = 2
EX = 16
EY = 32
NX = 128
NY = 256
NZ = 768


def expand_nodes(length_elems):
    position = jnp.arange((ORDER + 1) * length_elems, dtype=jnp.int32)
    return position // (ORDER + 1) * ORDER + position % (ORDER + 1)


def draw_fixed(key, part):
    unique = jax.random.randint(key, (ORDER * EX + 1, ORDER * EY + 1), 0, 2, dtype=jnp.int32)
    return unique[expand_nodes(EX)][:, expand_nodes(EY)]


def draw_rhs_loads(key, part):
    first_key, second_key = jax.random.split(key)
    across = jnp.arange(NX, dtype=jnp.float32) / NX
    element_scale = jnp.exp(jax.random.uniform(second_key, (EX, EY, EZ), jnp.float32, -0.7, 0.7))
    element_scale = jnp.repeat(jnp.repeat(jnp.repeat(element_scale, ORDER + 1, axis=0), ORDER + 1, axis=1), ORDER + 1, axis=2)
    noise_field = jax.random.normal(first_key, (3, NX, NY, NZ), jnp.float32)
    slope_scale = 1.0 + 2.0 * across
    values = noise_field * slope_scale[None, :, None, None] * element_scale[None]
    return jnp.clip(values, -16.0, 16.0).astype(jnp.float32)


def touch_ends(drawn, rng, smallest, largest):
    shape = drawn.shape
    index_at = [jax.random.randint(jax.random.fold_in(rng, axis), (), 0, shape[axis]) for axis in range(len(shape))]
    drawn = drawn.at[tuple(index_at)].set(smallest)
    longest = shape.index(max(shape))
    index_at[longest] = (index_at[longest] + 1) % shape[longest]
    return drawn.at[tuple(index_at)].set(largest)


def setup_inputs(seed: int = 0) -> dict:
    arg_keys = jax.random.split(jax.random.key(seed), 4)
    rhs_loads = draw_rhs_loads(jax.random.fold_in(arg_keys[3], 71), 0)
    flags = touch_ends(jax.random.randint(arg_keys[1], (EX, EY, EZ), 0, 2), jax.random.fold_in(arg_keys[1], 1), 0, 1).astype(jnp.int32)
    fixed = draw_fixed(jax.random.fold_in(arg_keys[3], 71), 0)
    return dict(rhs_loads=rhs_loads, flags=flags, fixed=fixed)


POISSON = 0.3
LAME_FIRST = POISSON / ((1.0 + POISSON) * (1.0 - 2.0 * POISSON))
LAME_SHEAR = 1.0 / (2.0 * (1.0 + POISSON))
SOLID_MODULUS = 0.1
VOID_MODULUS = 0.001
HIGHEST = lax.Precision.HIGHEST
INTERIOR_POINTS = (-0.8717401485096066, -0.5917001814331423, -0.2092992179024789, 0.2092992179024789, 0.5917001814331423, 0.8717401485096066)


def legendre_value(poly_order, point):
    previous = 1.0
    current = point
    for degree in range(1, poly_order):
        following = ((2.0 * degree + 1.0) * point * current - degree * previous) / (degree + 1.0)
        previous = current
        current = following
    return current


def gll_tables(poly_order):
    points = np.array([-1.0] + list(INTERIOR_POINTS) + [1.0])
    values = np.array([legendre_value(poly_order, float(point)) for point in points])
    weights = 2.0 / (poly_order * (poly_order + 1) * values ** 2)
    node_count = poly_order + 1
    derivative = np.zeros((node_count, node_count))
    for row_index in range(node_count):
        for col_index in range(node_count):
            if row_index != col_index:
                derivative[row_index, col_index] = values[row_index] / (values[col_index] * (points[row_index] - points[col_index]))
    derivative[0, 0] = -poly_order * (poly_order + 1) / 4.0
    derivative[poly_order, poly_order] = poly_order * (poly_order + 1) / 4.0
    return derivative, weights


def shared_halves(local_len, offset, global_len, node_count):
    position = jnp.arange(local_len, dtype=jnp.int32)
    node_index = position % node_count
    global_pos = position + offset
    shared = ((node_index == 0) & (global_pos > 0)) | ((node_index == node_count - 1) & (global_pos < global_len - 1))
    return jnp.where(shared, 0.5, 1.0).astype(jnp.float32)


def pair_core(padded, which_dim, node_count):
    inner_len = padded.shape[which_dim] - 2
    middle = lax.slice_in_dim(padded, 1, inner_len + 1, axis=which_dim)
    ahead = lax.slice_in_dim(padded, 2, inner_len + 2, axis=which_dim)
    behind = lax.slice_in_dim(padded, 0, inner_len, axis=which_dim)
    node_index = jnp.arange(inner_len) % node_count
    view_shape = tuple(inner_len if dim_index == which_dim else 1 for dim_index in range(padded.ndim))
    upper_node = (node_index == node_count - 1).reshape(view_shape)
    lower_node = (node_index == 0).reshape(view_shape)
    return middle + jnp.where(upper_node, ahead, 0.0) + jnp.where(lower_node, behind, 0.0)


def element_slab(displace, modulus, derivative, weight_cube):
    gradients = [
        jnp.einsum('ai,xifjgk->xafjgk', derivative, displace, precision=HIGHEST),
        jnp.einsum('bj,xifjgk->xifbgk', derivative, displace, precision=HIGHEST),
        jnp.einsum('ck,xifjgk->xifjgc', derivative, displace, precision=HIGHEST),
    ]
    shear_nodes = (modulus * LAME_SHEAR)[None, :, None, :, None] * weight_cube
    lame_nodes = (modulus * LAME_FIRST)[None, :, None, :, None] * weight_cube
    spread = gradients[0][0] + gradients[1][1] + gradients[2][2]
    summed = jnp.zeros_like(displace)
    for direction in range(3):
        mirror = jnp.stack([gradients[0][direction], gradients[1][direction], gradients[2][direction]])
        stress = shear_nodes * (gradients[direction] + mirror)
        stress = stress.at[direction].add(lame_nodes * spread)
        if direction == 0:
            summed = summed + jnp.einsum('ai,xafjgk->xifjgk', derivative, stress, precision=HIGHEST)
        elif direction == 1:
            summed = summed + jnp.einsum('bj,xifbgk->xifjgk', derivative, stress, precision=HIGHEST)
        else:
            summed = summed + jnp.einsum('ck,xifjgc->xifjgk', derivative, stress, precision=HIGHEST)
    return summed


def reference(rhs_loads, flags, fixed):
    node_count = ORDER + 1
    derivative_np, weights_np = gll_tables(ORDER)
    derivative = jnp.asarray(derivative_np, jnp.float32)
    weights = jnp.asarray(weights_np, jnp.float32)
    weight_cube = weights[:, None, None, None, None] * weights[None, None, :, None, None] * weights[None, None, None, None, :]
    modulus = jnp.where(flags == 1, SOLID_MODULUS, VOID_MODULUS).astype(jnp.float32)
    free = 1.0 - fixed.astype(jnp.float32)[:, :, None] * (jnp.arange(NZ) == 0).astype(jnp.float32)[None, None, :]
    weight_x = shared_halves(NX, 0, NX, node_count)
    weight_y = shared_halves(NY, 0, NY, node_count)
    weight_z = shared_halves(NZ, 0, NZ, node_count)

    def stiffness(values_in):
        slabs = values_in.reshape(3, EX, node_count, EY, node_count, EZ, node_count).transpose(1, 0, 2, 3, 4, 5, 6)

        def slab_apply(operands):
            return element_slab(operands[0], operands[1], derivative, weight_cube)

        result = lax.map(slab_apply, (slabs, modulus))
        return result.transpose(1, 0, 2, 3, 4, 5, 6).reshape(3, NX, NY, NZ)

    def assemble(values_in):
        summed = values_in
        for which_dim in (1, 2, 3):
            widths = [(0, 0)] * 4
            widths[which_dim] = (1, 1)
            summed = pair_core(jnp.pad(summed, widths), which_dim, node_count)
        return free[None] * summed

    def inner(first, second):
        return jnp.sum(first * second * weight_x[None, :, None, None] * weight_y[None, None, :, None] * weight_z[None, None, None, :])

    loads = assemble(rhs_loads)
    adjoint = jnp.zeros_like(loads)
    residual = loads
    direction = loads
    norm_now = inner(residual, residual)
    for turn_index in range(ITERS):
        image_vec = assemble(stiffness(direction))
        step_size = norm_now / inner(direction, image_vec)
        adjoint = adjoint + step_size * direction
        residual = residual - step_size * image_vec
        if turn_index + 1 < ITERS:
            norm_next = inner(residual, residual)
            direction = residual + (norm_next / norm_now) * direction
            norm_now = norm_next
    return adjoint, residual
```

```python
import functools

import jax
import jax.numpy as jnp
import numpy as np
from jax import lax
from jax.experimental import pallas as pl
from jax.experimental.pallas import tpu as pltpu
from jax.sharding import PartitionSpec as P

ORDER = 7
NODES = ORDER + 1
LANES = 128

POISSON = 0.3
LAME_FIRST = POISSON / ((1.0 + POISSON) * (1.0 - 2.0 * POISSON))
LAME_SHEAR = 1.0 / (2.0 * (1.0 + POISSON))
SOLID_MODULUS = 0.1
VOID_MODULUS = 0.001
HIGHEST = lax.Precision.HIGHEST
INTERIOR_POINTS = (
    -0.8717401485096066,
    -0.5917001814331423,
    -0.2092992179024789,
    0.2092992179024789,
    0.5917001814331423,
    0.8717401485096066,
)
VMEM_LIMIT = 40 * 1024 * 1024


def legendre_value(poly_order, point):
    previous = 1.0
    current = point
    for degree in range(1, poly_order):
        following = ((2.0 * degree + 1.0) * point * current - degree * previous) / (degree + 1.0)
        previous = current
        current = following
    return current


def gll_tables(poly_order):
    points = np.array([-1.0] + list(INTERIOR_POINTS) + [1.0])
    values = np.array([legendre_value(poly_order, float(point)) for point in points])
    weights = 2.0 / (poly_order * (poly_order + 1) * values**2)
    node_count = poly_order + 1
    derivative = np.zeros((node_count, node_count))
    for row_index in range(node_count):
        for col_index in range(node_count):
            if row_index != col_index:
                derivative[row_index, col_index] = values[row_index] / (
                    values[col_index] * (points[row_index] - points[col_index])
                )
    derivative[0, 0] = -poly_order * (poly_order + 1) / 4.0
    derivative[poly_order, poly_order] = poly_order * (poly_order + 1) / 4.0
    return (derivative, weights)


DERIV, WEIGHTS = gll_tables(ORDER)
HALF = NODES // 2
ODD = [[0.5 * (DERIV[a, i] - DERIV[a, ORDER - i]) for i in range(HALF)] for a in range(HALF)]
EVEN = [[0.5 * (DERIV[a, i] + DERIV[a, ORDER - i]) for i in range(HALF)] for a in range(HALF)]


def shared_halves(local_len, offset, global_len, node_count):
    position = jnp.arange(local_len, dtype=jnp.int32)
    node_index = position % node_count
    global_pos = position + offset
    shared = (node_index == 0) & (global_pos > 0) | (node_index == node_count - 1) & (
        global_pos < global_len - 1
    )
    return jnp.where(shared, 0.5, 1.0).astype(jnp.float32)


def combine(coefs, terms):
    total = None
    for coef, term in zip(coefs, terms):
        part = float(coef) * term
        total = part if total is None else total + part
    return total


def row_sum_y(v_ref, lo, hi, comp, plane, elem, n_elem):
    base = elem * NODES
    own = v_ref[comp, plane, base : base + NODES, :]
    below = lo if elem == 0 else v_ref[comp, plane, base - 1 : base, :]
    above = hi if elem == n_elem - 1 else v_ref[comp, plane, base + NODES : base + NODES + 1, :]
    sub = lax.broadcasted_iota(jnp.int32, own.shape, 0)
    below = jnp.broadcast_to(below, own.shape)
    above = jnp.broadcast_to(above, own.shape)
    return own + jnp.where(sub == 0, below, jnp.where(sub == ORDER, above, 0.0))


def sum_z(rows):
    size = rows.shape[-1]
    lane = lax.broadcasted_iota(jnp.int32, rows.shape, 1)
    ahead = pltpu.roll(rows, size - 1, 1)
    behind = pltpu.roll(rows, 1, 1)
    upper = (lane % NODES == ORDER) & (lane < size - 1)
    lower = (lane % NODES == 0) & (lane > 0)
    return rows + jnp.where(upper, ahead, jnp.where(lower, behind, 0.0))


def assembled_strip(v_ref, ylo_ref, yhi_ref, xlo_ref, xhi_ref, free_ref, comp, plane, elem, n_elem):
    lo = ylo_ref[comp, plane : plane + 1, :]
    hi = yhi_ref[comp, plane : plane + 1, :]
    rows = row_sum_y(v_ref, lo, hi, comp, plane, elem, n_elem)
    base = elem * NODES
    if plane == 0:
        rows = rows + xlo_ref[comp, base : base + NODES, :]
    if plane == ORDER:
        rows = rows + xhi_ref[comp, base : base + NODES, :]
    rows = sum_z(rows)
    head = rows[:, :LANES] * free_ref[plane, base : base + NODES, :]
    return jnp.concatenate([head, rows[:, LANES:]], axis=1)


def fold(strip):
    total = strip[:, :LANES]
    for start in range(LANES, strip.shape[1], LANES):
        total = total + strip[:, start : start + LANES]
    return total


def apply_kernel(
    v_ref, ylo_ref, yhi_ref, xlo_ref, xhi_ref, free_ref, elem_ref, half_ref, halfz_ref,
    zmat_ref, ycol_ref, sums_in_ref,
    u_ref, k_ref, flo_ref, fhi_ref, sums_ref,
    grad_ref, stress_ref, side_ref, *, slot,
):
    comps, planes, size_y, size_z = v_ref.shape
    n_elem = size_y // NODES
    n_tile = size_z // LANES
    square = jnp.zeros((NODES, LANES), jnp.float32)
    for elem in range(n_elem):
        base = elem * NODES
        for plane in range(planes):
            part = None
            for comp in range(comps):
                strip = assembled_strip(
                    v_ref, ylo_ref, yhi_ref, xlo_ref, xhi_ref, free_ref, comp, plane, elem, n_elem
                )
                u_ref[comp, plane, base : base + NODES, :] = strip
                part = strip * strip if part is None else part + strip * strip
            part = fold(part * halfz_ref[0:1, :])
            square = square + part * half_ref[plane, base : base + NODES, :]

    rows = comps * planes * size_y
    for tile in range(n_tile):
        lanes = slice(tile * LANES, (tile + 1) * LANES)
        flat = u_ref[:, :, :, lanes].reshape(rows, LANES)
        grad_ref[:, :, :, lanes] = jnp.dot(
            flat, zmat_ref[0], precision=HIGHEST, preferred_element_type=jnp.float32
        ).reshape(comps, planes, size_y, LANES)

    def block(tile, elem):
        lanes = pl.ds(pl.multiple_of(tile * LANES, LANES), LANES)
        base = elem * NODES
        sub = slice(base, base + NODES)
        even, odd = [], []
        for comp in range(3):
            vals = [u_ref[comp, i, sub, lanes] for i in range(NODES)]
            even.append([vals[i] + vals[ORDER - i] for i in range(HALF)])
            odd.append([vals[i] - vals[ORDER - i] for i in range(HALF)])
        scale = elem_ref[sub, lanes]
        xsum = [[None] * HALF for _ in range(3)]
        xdif = [[None] * HALF for _ in range(3)]
        for pair in range(HALF):
            first = [combine(ODD[pair], odd[c]) for c in range(3)]
            second = [combine(EVEN[pair], even[c]) for c in range(3)]
            side_x = []
            for plane, sign in ((pair, 1), (ORDER - pair, -1)):
                gx = [first[c] + second[c] if sign > 0 else first[c] - second[c] for c in range(3)]
                gy = []
                for c in range(3):
                    total = None
                    for j in range(NODES):
                        row = u_ref[c, plane, base + j : base + j + 1, lanes]
                        part = ycol_ref[0, j] * jnp.broadcast_to(row, (NODES, LANES))
                        total = part if total is None else total + part
                    gy.append(total)
                gz = [grad_ref[c, plane, sub, lanes] for c in range(3)]
                shear = scale * float(LAME_SHEAR * WEIGHTS[plane])
                twice = scale * float(2.0 * LAME_SHEAR * WEIGHTS[plane])
                spread = (gx[0] + gy[1] + gz[2]) * (scale * float(LAME_FIRST * WEIGHTS[plane]))
                sxx = twice * gx[0] + spread
                syy = twice * gy[1] + spread
                szz = twice * gz[2] + spread
                sxy = shear * (gx[1] + gy[0])
                sxz = shear * (gx[2] + gz[0])
                syz = shear * (gy[2] + gz[1])
                side_x.append((sxx, sxy, sxz))
                for c, value in enumerate((sxz, syz, szz)):
                    stress_ref[c, plane, sub, lanes] = value
                for c, value in enumerate((sxy, syy, syz)):
                    side_ref[c, plane, :, :] = value
            for c in range(3):
                se = side_x[0][c] + side_x[1][c]
                so = side_x[0][c] - side_x[1][c]
                for i in range(HALF):
                    add_x = float(EVEN[pair][i]) * so
                    add_y = float(ODD[pair][i]) * se
                    xsum[c][i] = add_x if pair == 0 else xsum[c][i] + add_x
                    xdif[c][i] = add_y if pair == 0 else xdif[c][i] + add_y
        for c in range(3):
            for plane in range(NODES):
                i = min(plane, ORDER - plane)
                total = xsum[c][i] + xdif[c][i] if plane < HALF else xsum[c][i] - xdif[c][i]
                for b in range(NODES):
                    row = side_ref[c, plane, b : b + 1, :]
                    total = total + ycol_ref[1, b] * jnp.broadcast_to(row, (NODES, LANES))
                k_ref[c, plane, sub, lanes] = total

    @pl.loop(0, n_tile)
    def _(tile):
        for elem in range(n_elem):
            block(tile, elem)

    energy = jnp.zeros((NODES, LANES), jnp.float32)
    for tile in range(n_tile):
        lanes = slice(tile * LANES, (tile + 1) * LANES)
        flat = stress_ref[:, :, :, lanes].reshape(rows, LANES)
        total = jnp.dot(
            flat, zmat_ref[1], precision=HIGHEST, preferred_element_type=jnp.float32
        ).reshape(comps, planes, size_y, LANES)
        total = total + k_ref[:, :, :, lanes]
        k_ref[:, :, :, lanes] = total
        product = (total * u_ref[:, :, :, lanes]).reshape(rows // NODES, NODES, LANES)
        energy = energy + jnp.sum(product, axis=0)
    for comp in range(comps):
        for plane in range(planes):
            flo_ref[comp, plane : plane + 1, :] = k_ref[comp, plane, 0:1, :]
            fhi_ref[comp, plane : plane + 1, :] = k_ref[comp, plane, size_y - 1 : size_y, :]
    lane = lax.broadcasted_iota(jnp.int32, sums_ref.shape, 1)
    known = jnp.zeros(sums_ref.shape, jnp.float32) if slot == 0 else sums_in_ref[...]
    known = jnp.where(lane == 2 * slot, jnp.sum(square), known)
    sums_ref[...] = jnp.where(lane == 2 * slot + 1, jnp.sum(energy), known)


def rows_kernel(v_ref, lo_ref, hi_ref):
    comps, planes, size_y, _ = v_ref.shape
    for comp in range(comps):
        for plane in range(planes):
            lo_ref[comp, plane : plane + 1, :] = v_ref[comp, plane, 0:1, :]
            hi_ref[comp, plane : plane + 1, :] = v_ref[comp, plane, size_y - 1 : size_y, :]


def faces_kernel(vlo_ref, vhi_ref, ylo_ref, yhi_ref, xlo_ref, xhi_ref):
    comps, _, size_y, _ = vlo_ref.shape
    n_elem = size_y // NODES
    for v_ref, plane, out_ref in ((vlo_ref, 0, xlo_ref), (vhi_ref, ORDER, xhi_ref)):
        for comp in range(comps):
            lo = ylo_ref[comp, plane : plane + 1, :]
            hi = yhi_ref[comp, plane : plane + 1, :]
            for elem in range(n_elem):
                base = elem * NODES
                out_ref[comp, base : base + NODES, :] = row_sum_y(
                    v_ref, lo, hi, comp, 0, elem, n_elem
                )


def finish_kernel(
    k_ref, ylo_ref, yhi_ref, xlo_ref, xhi_ref, free_ref, r_ref, q_ref, sums_ref, adj_ref, res_ref
):
    comps, planes, size_y, _ = k_ref.shape
    n_elem = size_y // NODES
    sums = jnp.sum(sums_ref[...], axis=0, keepdims=True)
    lane = lax.broadcasted_iota(jnp.int32, sums.shape, 1)
    m0, m1, m2, m3 = [
        jnp.sum(jnp.where(lane == i, sums, 0.0), axis=1, keepdims=True) for i in range(4)
    ]
    first = m0 / m1
    following = first * first * m2 - m0
    ratio = following / m0
    grow = 1.0 + ratio
    second = following / (grow * grow * m1 - 2.0 * first * grow * m2 + first * first * m3)
    lead = first + second * grow
    cross = first * second
    for elem in range(n_elem):
        base = elem * NODES
        sub = slice(base, base + NODES)
        for plane in range(planes):
            for comp in range(comps):
                strip = assembled_strip(
                    k_ref, ylo_ref, yhi_ref, xlo_ref, xhi_ref, free_ref, comp, plane, elem, n_elem
                )
                loads = r_ref[comp, plane, sub, :]
                image = q_ref[comp, plane, sub, :]
                adj_ref[comp, plane, sub, :] = lead * loads - cross * image
                res_ref[comp, plane, sub, :] = loads - lead * image + cross * strip


def halo(low_side, high_side, axis):
    count = lax.axis_size(axis)
    forward = [(i, i + 1) for i in range(count - 1)]
    backward = [(target, source) for source, target in forward]
    return lax.ppermute(high_side, axis, forward), lax.ppermute(low_side, axis, backward)


def local(rhs_loads, flags, fixed):
    comps, size_x, size_y, size_z = rhs_loads.shape
    axes = ("gx", "gy")
    devices = lax.axis_size("gx") * lax.axis_size("gy")
    params = pltpu.CompilerParams(vmem_limit_bytes=VMEM_LIMIT)
    f32 = jnp.float32
    field = jax.ShapeDtypeStruct(rhs_loads.shape, f32)
    y_side = jax.ShapeDtypeStruct((comps, size_x, size_z), f32)
    x_side = jax.ShapeDtypeStruct((comps, size_y, size_z), f32)
    whole = pl.BlockSpec(memory_space=pltpu.VMEM)

    modulus = jnp.where(flags[0] == 1, SOLID_MODULUS, VOID_MODULUS).astype(f32)
    modulus = jnp.repeat(jnp.repeat(modulus, NODES, axis=0), NODES, axis=1)
    weight_y = jnp.asarray(np.tile(WEIGHTS, size_y // NODES), f32)
    weight_z = jnp.asarray(np.tile(WEIGHTS, size_z // NODES), f32)
    elem_scale = modulus * weight_y[:, None] * weight_z[None, :]
    free = 1.0 - fixed.astype(f32)[:, :, None] * (jnp.arange(LANES) == 0).astype(f32)
    half_xy = (
        shared_halves(size_x, lax.axis_index("gx") * size_x, size_x * lax.axis_size("gx"), NODES)[
            :, None, None
        ]
        * shared_halves(
            size_y, lax.axis_index("gy") * size_y, size_y * lax.axis_size("gy"), NODES
        )[None, :, None]
        * jnp.ones((LANES,), f32)
    )
    half_z = jnp.broadcast_to(shared_halves(size_z, 0, size_z, NODES)[None], (NODES, size_z))
    z_mat = jnp.asarray(
        np.stack([np.kron(np.eye(LANES // NODES), m) for m in (DERIV.T, DERIV)]), f32
    )
    y_col = jnp.asarray(
        np.broadcast_to(
            np.stack([DERIV.T, DERIV])[:, :, :, None], (2, NODES, NODES, LANES)
        ),
        f32,
    )

    def faces(v, ylo, yhi):
        block = (comps, 1, size_y, size_z)
        side = pl.BlockSpec((comps, size_x, size_z), lambda i: (0, 0, 0))
        out = pl.BlockSpec((comps, size_y, size_z), lambda i: (0, 0, 0))
        return pl.pallas_call(
            faces_kernel,
            grid=(1,),
            in_specs=[
                pl.BlockSpec(block, lambda i: (0, 0, 0, 0)),
                pl.BlockSpec(block, lambda i: (0, size_x - 1, 0, 0)),
                side,
                side,
            ],
            out_specs=[out, out],
            out_shape=[x_side, x_side],
            compiler_params=params,
            name="faces",
        )(v, v, ylo, yhi)

    def apply_stiffness(v, halos, sums, slot):
        return pl.pallas_call(
            functools.partial(apply_kernel, slot=slot),
            in_specs=[whole] * 12,
            out_specs=[whole] * 5,
            out_shape=[
                field, field, y_side, y_side, jax.ShapeDtypeStruct((devices, LANES), f32)
            ],
            scratch_shapes=[
                pltpu.VMEM(rhs_loads.shape, f32),
                pltpu.VMEM(rhs_loads.shape, f32),
                pltpu.VMEM((comps, size_x, NODES, LANES), f32),
            ],
            compiler_params=params,
            name="stiffness",
        )(v, *halos, free, elem_scale, half_xy, half_z, z_mat, y_col, sums)

    def exchange(v, low_rows, high_rows):
        ylo, yhi = halo(low_rows, high_rows, "gy")
        xlo, xhi = halo(*faces(v, ylo, yhi), "gx")
        return ylo, yhi, xlo, xhi

    low_rows, high_rows = pl.pallas_call(
        rows_kernel,
        in_specs=[whole],
        out_specs=[whole] * 2,
        out_shape=[y_side, y_side],
        compiler_params=params,
        name="rows",
    )(rhs_loads)
    sums = jnp.zeros((devices, LANES), f32)
    halos = exchange(rhs_loads, low_rows, high_rows)
    loads, k_loads, low_rows, high_rows, sums = apply_stiffness(rhs_loads, halos, sums, 0)
    halos = exchange(k_loads, low_rows, high_rows)
    image, k_image, low_rows, high_rows, sums = apply_stiffness(k_loads, halos, sums, 1)
    halos = exchange(k_image, low_rows, high_rows)
    sums = lax.all_to_all(sums, axes, 0, 0, tiled=True)
    return tuple(
        pl.pallas_call(
            finish_kernel,
            in_specs=[whole] * 9,
            out_specs=[whole] * 2,
            out_shape=[field, field],
            compiler_params=params,
            name="finish",
        )(k_image, *halos, free, loads, image, sums)
    )


def solution(mesh):
    in_specs = (P(None, "gx", "gy", None), P("gx", "gy", None), P("gx", "gy"))
    out_specs = (P(None, "gx", "gy", None), P(None, "gx", "gy", None))
    return jax.shard_map(local, mesh=mesh, in_specs=in_specs, out_specs=out_specs, check_vma=False)
```

```python
import functools

import jax
import jax.numpy as jnp
import numpy as np
from jax import lax
from jax.experimental import pallas as pl
from jax.experimental.pallas import tpu as pltpu
from jax.sharding import PartitionSpec as P

ORDER = 7
NODES = ORDER + 1
LANES = 128

POISSON = 0.3
LAME_FIRST = POISSON / ((1.0 + POISSON) * (1.0 - 2.0 * POISSON))
LAME_SHEAR = 1.0 / (2.0 * (1.0 + POISSON))
SOLID_MODULUS = 0.1
VOID_MODULUS = 0.001
INTERIOR_POINTS = (
    -0.8717401485096066,
    -0.5917001814331423,
    -0.2092992179024789,
    0.2092992179024789,
    0.5917001814331423,
    0.8717401485096066,
)
VMEM_LIMIT = 16 * 1024 * 1024


def legendre_value(poly_order, point):
    previous = 1.0
    current = point
    for degree in range(1, poly_order):
        following = ((2.0 * degree + 1.0) * point * current - degree * previous) / (degree + 1.0)
        previous = current
        current = following
    return current


def gll_tables(poly_order):
    points = np.array([-1.0] + list(INTERIOR_POINTS) + [1.0])
    values = np.array([legendre_value(poly_order, float(point)) for point in points])
    weights = 2.0 / (poly_order * (poly_order + 1) * values**2)
    node_count = poly_order + 1
    derivative = np.zeros((node_count, node_count))
    for row_index in range(node_count):
        for col_index in range(node_count):
            if row_index != col_index:
                derivative[row_index, col_index] = values[row_index] / (
                    values[col_index] * (points[row_index] - points[col_index])
                )
    derivative[0, 0] = -poly_order * (poly_order + 1) / 4.0
    derivative[poly_order, poly_order] = poly_order * (poly_order + 1) / 4.0
    return (derivative, weights)


DERIV, WEIGHTS = gll_tables(ORDER)
HALF = NODES // 2
ODD = [[0.5 * (DERIV[a, i] - DERIV[a, ORDER - i]) for i in range(HALF)] for a in range(HALF)]
EVEN = [[0.5 * (DERIV[a, i] + DERIV[a, ORDER - i]) for i in range(HALF)] for a in range(HALF)]


def z_table(matrix):
    blocks = np.kron(np.eye(LANES // NODES), matrix).astype(np.float32)
    high = blocks.astype(jnp.bfloat16)
    low = (blocks - high.astype(np.float32)).astype(jnp.bfloat16)
    row = np.concatenate([high, low], axis=1)
    return np.concatenate([row, row], axis=0)


def shared_halves(local_len, offset, global_len, node_count):
    position = jnp.arange(local_len, dtype=jnp.int32)
    node_index = position % node_count
    global_pos = position + offset
    shared = (node_index == 0) & (global_pos > 0) | (node_index == node_count - 1) & (
        global_pos < global_len - 1
    )
    return jnp.where(shared, 0.5, 1.0).astype(jnp.float32)


def combine(coefs, terms):
    total = None
    for coef, term in zip(coefs, terms):
        part = float(coef) * term
        total = part if total is None else total + part
    return total


def parts(n_elem):
    return tuple(range(1, n_elem - 1)), (0, n_elem - 1)


def locate(refs, elem, n_elem):
    if refs[0].shape[2] == n_elem * NODES:
        return refs[0], elem * NODES
    for ref, group in zip(refs, parts(n_elem)):
        if elem in group:
            return ref, group.index(elem) * NODES


def row_sum_y(refs, lo, hi, comp, plane, elem, n_elem):
    ref, base = locate(refs, elem, n_elem)
    own = ref[comp, plane, base : base + NODES, :]
    if elem > 0:
        ref, base = locate(refs, elem - 1, n_elem)
        lo = ref[comp, plane, base + ORDER : base + NODES, :]
    if elem < n_elem - 1:
        ref, base = locate(refs, elem + 1, n_elem)
        hi = ref[comp, plane, base : base + 1, :]
    sub = lax.broadcasted_iota(jnp.int32, own.shape, 0)
    lo = jnp.broadcast_to(lo, own.shape)
    hi = jnp.broadcast_to(hi, own.shape)
    return own + jnp.where(sub == 0, lo, jnp.where(sub == ORDER, hi, 0.0))


def sum_z(rows):
    size = rows.shape[-1]
    lane = lax.broadcasted_iota(jnp.int32, rows.shape, 1)
    ahead = pltpu.roll(rows, size - 1, 1)
    behind = pltpu.roll(rows, 1, 1)
    upper = (lane % NODES == ORDER) & (lane < size - 1)
    lower = (lane % NODES == 0) & (lane > 0)
    return rows + jnp.where(upper, ahead, jnp.where(lower, behind, 0.0))


def release(rows, free):
    return jnp.concatenate([rows[:, :LANES] * free, rows[:, LANES:]], axis=1)


def fold(strip):
    total = strip[:, :LANES]
    for start in range(LANES, strip.shape[1], LANES):
        total = total + strip[:, start : start + LANES]
    return total


def is_upper(axis):
    return lax.axis_index(axis) % 2


def pick(upper, near, far):
    mask = jnp.full(near.shape, upper, jnp.int32) == 1
    return jnp.where(mask, near, far), jnp.where(mask, far, near)


def y_sides(upper, near_ref, far_ref, comp, plane):
    row = slice(plane, plane + 1)
    return pick(upper, near_ref[comp, row, :], far_ref[comp, row, :])


def column_sum(y_col_ref, which, row_of):
    total = None
    for j in range(NODES):
        part = y_col_ref[which, j] * jnp.broadcast_to(row_of(j), (NODES, LANES))
        total = part if total is None else total + part
    return total


def along_z(flat, table):
    high = flat.astype(jnp.bfloat16)
    low = (flat - high.astype(jnp.float32)).astype(jnp.bfloat16)
    both = jnp.dot(
        jnp.concatenate([high, low], axis=1), table, preferred_element_type=jnp.float32
    )
    return both[:, :LANES] + both[:, LANES:]


def main_kernel(*refs, elems, n_elem):
    v_refs, refs = refs[:2], refs[2:]
    if 0 in elems:
        ynear_ref, yfar_ref = refs[:2]
        refs = refs[2:]
    free_ref, elem_ref, half_ref, halfz_ref, zmat_ref, ycol_ref = refs[:6]
    u_ref, k_ref, square_ref = refs[6:9]
    grad_ref, stress_ref, side_ref = refs[9:]
    comps, planes, size_y, size_z = u_ref.shape
    n_tile = size_z // LANES
    y_upper = is_upper("gy")
    square = jnp.zeros((NODES, LANES), jnp.float32)
    for place, elem in enumerate(elems):
        base = elem * NODES
        sub = slice(place * NODES, (place + 1) * NODES)
        for plane in range(planes):
            part = None
            for comp in range(comps):
                lo = hi = None
                if elem in (0, n_elem - 1):
                    lo, hi = y_sides(y_upper, ynear_ref, yfar_ref, comp, plane)
                strip = sum_z(row_sum_y(v_refs, lo, hi, comp, plane, elem, n_elem))
                strip = release(strip, free_ref[plane, base : base + NODES, :])
                u_ref[comp, plane, sub, :] = strip
                part = strip * strip if part is None else part + strip * strip
            if plane not in (0, ORDER):
                part = fold(part * halfz_ref[0:1, :])
                square = square + part * half_ref[plane, base : base + NODES, :]
    square_ref[...] = square

    rows = comps * planes * size_y
    for tile in range(n_tile):
        lanes = slice(tile * LANES, (tile + 1) * LANES)
        flat = u_ref[:, :, :, lanes].reshape(rows, LANES)
        grad_ref[:, :, :, lanes] = along_z(flat, zmat_ref[0]).reshape(
            comps, planes, size_y, LANES
        )

    def block(tile, place):
        lanes = pl.ds(pl.multiple_of(tile * LANES, LANES), LANES)
        base = place * NODES
        sub = slice(base, base + NODES)
        even, odd = [], []
        for comp in range(3):
            vals = [u_ref[comp, i, sub, lanes] for i in range(NODES)]
            even.append([vals[i] + vals[ORDER - i] for i in range(HALF)])
            odd.append([vals[i] - vals[ORDER - i] for i in range(HALF)])
        scale = elem_ref[elems[place] * NODES : (elems[place] + 1) * NODES, lanes]
        xsum = [[None] * HALF for _ in range(3)]
        xdif = [[None] * HALF for _ in range(3)]
        for pair in range(HALF):
            first = [combine(ODD[pair], odd[c]) for c in range(3)]
            second = [combine(EVEN[pair], even[c]) for c in range(3)]
            side_x = []
            for plane, sign in ((pair, 1), (ORDER - pair, -1)):
                gx = [first[c] + second[c] if sign > 0 else first[c] - second[c] for c in range(3)]
                gy = [
                    column_sum(
                        ycol_ref, 0, lambda j: u_ref[c, plane, base + j : base + j + 1, lanes]
                    )
                    for c in range(3)
                ]
                gz = [grad_ref[c, plane, sub, lanes] for c in range(3)]
                shear = scale * float(LAME_SHEAR * WEIGHTS[plane])
                twice = scale * float(2.0 * LAME_SHEAR * WEIGHTS[plane])
                spread = (gx[0] + gy[1] + gz[2]) * (scale * float(LAME_FIRST * WEIGHTS[plane]))
                sxx = twice * gx[0] + spread
                syy = twice * gy[1] + spread
                szz = twice * gz[2] + spread
                sxy = shear * (gx[1] + gy[0])
                sxz = shear * (gx[2] + gz[0])
                syz = shear * (gy[2] + gz[1])
                side_x.append((sxx, sxy, sxz))
                for c, value in enumerate((sxz, syz, szz)):
                    stress_ref[c, plane, sub, lanes] = value
                for c, value in enumerate((sxy, syy, syz)):
                    side_ref[c, plane, :, :] = value
            for c in range(3):
                se = side_x[0][c] + side_x[1][c]
                so = side_x[0][c] - side_x[1][c]
                for i in range(HALF):
                    add_x = float(EVEN[pair][i]) * so
                    add_y = float(ODD[pair][i]) * se
                    xsum[c][i] = add_x if pair == 0 else xsum[c][i] + add_x
                    xdif[c][i] = add_y if pair == 0 else xdif[c][i] + add_y
        for c in range(3):
            for plane in range(NODES):
                i = min(plane, ORDER - plane)
                total = xsum[c][i] + xdif[c][i] if plane < HALF else xsum[c][i] - xdif[c][i]
                k_ref[c, plane, sub, lanes] = total + column_sum(
                    ycol_ref, 1, lambda b: side_ref[c, plane, b : b + 1, :]
                )

    @pl.loop(0, n_tile)
    def _(tile):
        for place in range(len(elems)):
            block(tile, place)

    for tile in range(n_tile):
        lanes = slice(tile * LANES, (tile + 1) * LANES)
        flat = stress_ref[:, :, :, lanes].reshape(rows, LANES)
        k_ref[:, :, :, lanes] += along_z(flat, zmat_ref[1]).reshape(comps, planes, size_y, LANES)


SHEAR, FIRST = float(LAME_SHEAR), float(LAME_FIRST)
DIAG = 2.0 * SHEAR + FIRST
ENDS = (0, ORDER)
THROUGH = np.einsum("ai,a,ap->ip", DERIV, WEIGHTS, DERIV)
ONWARD = DERIV.T
BACKWARD = WEIGHTS[:, None] * DERIV


def spread_pair(total_p, total_m, table, i, sign, even, odd):
    alpha = 0.5 * float(table[i, 0] + table[i, ORDER]) * even
    beta = 0.5 * float(table[i, 0] - table[i, ORDER]) * odd
    plus, minus = (alpha, beta) if sign > 0 else (beta, alpha)
    if total_p is None:
        return plus, minus
    return total_p + plus, total_m + minus


def update_kernel(*refs, elems, n_elem, slot, last):
    u_ref, kin_ref, xnear_ref, xfar_ref = refs[:4]
    free_ref, elem_ref, half_ref, halfz_ref, zmat_ref, ycol_ref = refs[4:10]
    squares_refs, refs = (refs[10:12], refs[12:]) if 0 in elems else ((), refs[10:])
    carry_ref, k_ref, face_ref, sums_ref = refs[:4]
    refs = refs[4:]
    if 0 in elems:
        near_ref, far_ref = refs[:2]
        refs = refs[2:]
    add_ref, grad_ref, keep_ref, zin_ref, zout_ref, side_ref = refs
    comps, planes, size_y, size_z = k_ref.shape
    n_tile = size_z // LANES
    x_upper = is_upper("gx")
    square = jnp.zeros((NODES, LANES), jnp.float32)
    for ref in squares_refs:
        square = square + ref[...]
    for place, elem in enumerate(elems):
        rows = slice(elem * NODES, (elem + 1) * NODES)
        own = slice(place * NODES, (place + 1) * NODES)
        for end, plane in enumerate(ENDS):
            part = None
            for comp in range(comps):
                strip = pick(x_upper, xnear_ref[comp, rows, :], xfar_ref[comp, rows, :])[end]
                strip = release(sum_z(strip), free_ref[plane, rows, :])
                add_ref[comp, end, own, :] = strip
                strip = strip + u_ref[comp, plane, own, :]
                face_ref[comp, end, own, :] = strip
                part = strip * strip if part is None else part + strip * strip
            square = square + fold(part * halfz_ref[0:1, :]) * half_ref[plane, rows, :]

    for tile in range(n_tile):
        lanes = slice(tile * LANES, (tile + 1) * LANES)
        flat = add_ref[:, :, :, lanes].reshape(comps * 2 * size_y, LANES)
        grad_ref[:, :, :, lanes] = along_z(flat, zmat_ref[0]).reshape(comps, 2, size_y, LANES)

    @pl.loop(0, n_tile)
    def _(tile):
        lanes = pl.ds(pl.multiple_of(tile * LANES, LANES), LANES)
        for place, elem in enumerate(elems):
            base = place * NODES
            sub = slice(base, base + NODES)
            scale = elem_ref[elem * NODES : (elem + 1) * NODES, lanes]
            for end, plane in enumerate(ENDS):
                gy = [
                    column_sum(
                        ycol_ref, 0, lambda j: add_ref[c, end, base + j : base + j + 1, lanes]
                    )
                    for c in range(3)
                ]
                gz = [grad_ref[c, end, sub, lanes] for c in range(3)]
                own = scale * float(WEIGHTS[plane])
                axx = own * (FIRST * (gy[1] + gz[2]))
                axy = own * (SHEAR * gy[0])
                axz = own * (SHEAR * gz[0])
                ayy = own * (DIAG * gy[1] + FIRST * gz[2])
                azz = own * (DIAG * gz[2] + FIRST * gy[1])
                ayz = own * (SHEAR * (gy[2] + gz[1]))
                scaled = [scale * add_ref[c, end, sub, lanes] for c in range(3)]
                for c, value in enumerate((SHEAR * scaled[2], FIRST * scaled[0], axz, ayz, azz)):
                    zin_ref[c, end, sub, lanes] = value
                for c, value in enumerate((SHEAR * scaled[1], FIRST * scaled[0], axy, ayy, ayz)):
                    side_ref[c, end, :, :] = value
                for c, value in enumerate((axx, axy, axz)):
                    keep_ref[c, end, sub, lanes] = value
                for c in range(5):
                    keep_ref[3 + c, end, sub, lanes] = column_sum(
                        ycol_ref, 1, lambda b: side_ref[c, end, b : b + 1, :]
                    )

    for tile in range(n_tile):
        lanes = slice(tile * LANES, (tile + 1) * LANES)
        flat = zin_ref[:, :, :, lanes].reshape(5 * 2 * size_y, LANES)
        zout_ref[:, :, :, lanes] = along_z(flat, zmat_ref[1]).reshape(5, 2, size_y, LANES)

    def tile_energy(tile, energy):
        lanes = pl.ds(pl.multiple_of(tile * LANES, LANES), LANES)
        for place, elem in enumerate(elems):
            sub = slice(place * NODES, (place + 1) * NODES)
            scale = elem_ref[elem * NODES : (elem + 1) * NODES, lanes]
            zout = [[zout_ref[c, end, sub, lanes] for end in range(2)] for c in range(5)]
            kept = [[keep_ref[c, end, sub, lanes] for end in range(2)] for c in range(8)]
            back = (
                [kept[3][end] + zout[0][end] for end in range(2)],
                kept[4],
                zout[1],
            )
            for c in range(3):
                factor = scale * (DIAG if c == 0 else SHEAR)
                pairs = (
                    ([factor * add_ref[c, end, sub, lanes] for end in range(2)], THROUGH, 1),
                    (kept[c], ONWARD, -1),
                    (back[c], BACKWARD, -1),
                )
                pairs = [(v[0] + v[1], v[0] - v[1], table, sign) for v, table, sign in pairs]
                for i in range(HALF):
                    plus = minus = None
                    for even, odd, table, sign in pairs:
                        plus, minus = spread_pair(plus, minus, table, i, sign, even, odd)
                    for plane, value in ((i, plus + minus), (ORDER - i, plus - minus)):
                        value = value + kin_ref[c, plane, sub, lanes]
                        if plane in ENDS:
                            end = ENDS.index(plane)
                            value = value + (kept[5 + c][end] + zout[2 + c][end])
                            vector = face_ref[c, end, sub, lanes]
                        else:
                            vector = u_ref[c, plane, sub, lanes]
                        k_ref[c, plane, sub, lanes] = value
                        energy = energy + value * vector
        return energy

    energy = lax.fori_loop(0, n_tile, tile_energy, jnp.zeros((NODES, LANES), jnp.float32))
    if 0 in elems:
        put_rows(
            lambda comp, plane: k_ref[comp, plane, 0:1, :],
            lambda comp, plane: k_ref[comp, plane, size_y - 1 : size_y, :],
            near_ref,
            far_ref,
        )
    moments = [carry_ref[i] for i in range(4)]
    moments[2 * slot] = moments[2 * slot] + square
    moments[2 * slot + 1] = moments[2 * slot + 1] + energy
    if not last:
        for i in range(4):
            sums_ref[i] = moments[i]
    else:
        lane = lax.broadcasted_iota(jnp.int32, sums_ref.shape, 1)
        known = jnp.zeros(sums_ref.shape, jnp.float32)
        for i in range(4):
            known = jnp.where(lane == i, jnp.sum(moments[i]), known)
        sums_ref[...] = known


def put_rows(lo_of, hi_of, near_ref, far_ref):
    y_upper = is_upper("gy")
    comps, planes, _ = near_ref.shape
    for comp in range(comps):
        for plane in range(planes):
            row = slice(plane, plane + 1)
            far_ref[comp, row, :], near_ref[comp, row, :] = pick(
                y_upper, hi_of(comp, plane), lo_of(comp, plane)
            )


def rows_kernel(v_ref, near_ref, far_ref):
    size_y = v_ref.shape[2]
    put_rows(
        lambda comp, plane: v_ref[comp, plane, 0:1, :],
        lambda comp, plane: v_ref[comp, plane, size_y - 1 : size_y, :],
        near_ref,
        far_ref,
    )


def faces_kernel(vmid_ref, vedge_ref, ynear_ref, yfar_ref, near_ref, far_ref):
    comps, size_y, _ = near_ref.shape
    n_elem = size_y // NODES
    x_upper, y_upper = is_upper("gx"), is_upper("gy")
    v_refs = vmid_ref, vedge_ref
    for comp in range(comps):
        sides = [y_sides(y_upper, ynear_ref, yfar_ref, comp, plane) for plane in ENDS]
        for elem in range(n_elem):
            rows = slice(elem * NODES, (elem + 1) * NODES)
            lo, hi = [
                row_sum_y(v_refs, *side, comp, plane, elem, n_elem)
                for plane, side in zip(ENDS, sides)
            ]
            near_ref[comp, rows, :], far_ref[comp, rows, :] = pick(x_upper, lo, hi)


def finish_kernel(*refs):
    k_refs = refs[:2]
    ynear_ref, yfar_ref, xnear_ref, xfar_ref, free_ref = refs[2:7]
    r_refs, r_faces, q_refs, q_faces = refs[7:9], refs[9:11], refs[11:13], refs[13:15]
    sums_ref, adj_out, res_out, adj_ref, res_ref, sem_ref = refs[15:]
    planes, comps, size_y, _ = adj_ref.shape
    n_elem = size_y // NODES
    x_upper, y_upper = is_upper("gx"), is_upper("gy")
    sums = jnp.sum(sums_ref[...], axis=0, keepdims=True)
    lane = lax.broadcasted_iota(jnp.int32, sums.shape, 1)
    m0, m1, m2, m3 = [
        jnp.sum(jnp.where(lane == i, sums, 0.0), axis=1, keepdims=True) for i in range(4)
    ]
    first = m0 / m1
    following = first * first * m2 - m0
    ratio = following / m0
    grow = 1.0 + ratio
    second = following / (grow * grow * m1 - 2.0 * first * grow * m2 + first * first * m3)
    lead = first + second * grow
    cross = first * second
    copies = []
    for plane in range(planes):
        for elem in range(n_elem):
            sub = slice(elem * NODES, (elem + 1) * NODES)
            end = ENDS.index(plane) if plane in ENDS else None
            place = plane if end is None else end
            r_ref, row = locate(r_refs if end is None else r_faces, elem, n_elem)
            q_ref, row = locate(q_refs if end is None else q_faces, elem, n_elem)
            own = slice(row, row + NODES)
            for comp in range(comps):
                lo = hi = None
                if elem in (0, n_elem - 1):
                    lo, hi = y_sides(y_upper, ynear_ref, yfar_ref, comp, plane)
                strip = row_sum_y(k_refs, lo, hi, comp, plane, elem, n_elem)
                if end is not None:
                    strip = strip + pick(x_upper, xnear_ref[comp, sub, :], xfar_ref[comp, sub, :])[end]
                loads = r_ref[comp, place, own, :]
                image = q_ref[comp, place, own, :]
                strip = release(sum_z(strip), free_ref[plane, sub, :])
                adj_ref[plane, comp, sub, :] = lead * loads - cross * image
                res_ref[plane, comp, sub, :] = loads - lead * image + cross * strip
        for which, (ref, out) in enumerate(((adj_ref, adj_out), (res_ref, res_out))):
            copy = pltpu.make_async_copy(ref.at[plane], out.at[:, plane], sem_ref.at[which, plane])
            copy.start()
            copies.append(copy)
    for copy in copies:
        copy.wait()


def swap(near_out, far_out, axis):
    count = lax.axis_size(axis)
    inner = [(i, i ^ 1) for i in range(count)]
    outer = [(i, ((i + 1) ^ 1) - 1) for i in range(1, count - 1)]
    far = lax.ppermute(far_out, axis, outer)
    near = lax.ppermute(near_out, axis, inner)
    return near, far


def local(rhs_loads, flags, fixed):
    comps, size_x, size_y, size_z = rhs_loads.shape
    axes = ("gx", "gy")
    devices = lax.axis_size("gx") * lax.axis_size("gy")
    f32 = jnp.float32
    y_side = jax.ShapeDtypeStruct((comps, size_x, size_z), f32)
    x_side = jax.ShapeDtypeStruct((comps, size_y, size_z), f32)
    whole = pl.BlockSpec(memory_space=pltpu.VMEM)

    modulus = jnp.where(flags[0] == 1, SOLID_MODULUS, VOID_MODULUS).astype(f32)
    modulus = jnp.repeat(jnp.repeat(modulus, NODES, axis=0), NODES, axis=1)
    weight_y = jnp.asarray(np.tile(WEIGHTS, size_y // NODES), f32)
    weight_z = jnp.asarray(np.tile(WEIGHTS, size_z // NODES), f32)
    elem_scale = modulus * weight_y[:, None] * weight_z[None, :]
    free = 1.0 - fixed.astype(f32)[:, :, None] * (jnp.arange(LANES) == 0).astype(f32)
    half_xy = (
        shared_halves(size_x, lax.axis_index("gx") * size_x, size_x * lax.axis_size("gx"), NODES)[
            :, None, None
        ]
        * shared_halves(
            size_y, lax.axis_index("gy") * size_y, size_y * lax.axis_size("gy"), NODES
        )[None, :, None]
        * jnp.ones((LANES,), f32)
    )
    half_z = jnp.broadcast_to(shared_halves(size_z, 0, size_z, NODES)[None], (NODES, size_z))
    z_mat = jnp.asarray(np.stack([z_table(DERIV.T), z_table(DERIV)]))
    y_col = jnp.asarray(
        np.broadcast_to(
            np.stack([DERIV.T, DERIV])[:, :, :, None], (2, NODES, NODES, LANES)
        ),
        f32,
    )

    n_elem = size_y // NODES
    mid, edge = parts(n_elem)
    tables = (free, elem_scale, half_xy, half_z, z_mat, y_col)

    def shape(*sizes):
        return jax.ShapeDtypeStruct(sizes, f32)

    def call(
        kernel, name, args, out_shape, scratch=(), us=1.0, out_spec=whole
    ):
        return pl.pallas_call(
            kernel,
            in_specs=[whole] * len(args),
            out_specs=[out_spec] * len(out_shape),
            out_shape=list(out_shape),
            scratch_shapes=list(scratch),
            compiler_params=pltpu.CompilerParams(vmem_limit_bytes=VMEM_LIMIT),
            cost_estimate=pl.CostEstimate(
                flops=int(us * 4e6), bytes_accessed=int(us * 2.5e6), transcendentals=0
            ),
            name=name,
        )(*args)

    def main(v, y_halo, elems, name):
        some = (comps, size_x, len(elems) * NODES, size_z)
        return call(
            functools.partial(main_kernel, elems=elems, n_elem=n_elem),
            name,
            (*v, *y_halo, *tables),
            (shape(*some), shape(*some), shape(NODES, LANES)),
            (
                pltpu.VMEM(some, f32),
                pltpu.VMEM(some, f32),
                pltpu.VMEM((comps, size_x, NODES, LANES), f32),
            ),
            us=5.0,
        )

    def update(u, k, x_halo, squares, carry, elems, slot, name):
        rows = len(elems) * NODES
        last = slot == 1 and 0 not in elems
        out = [
            shape(comps, size_x, rows, size_z),
            shape(comps, 2, rows, size_z),
            shape(devices, LANES) if last else shape(4, NODES, LANES),
        ]
        if 0 in elems:
            out += [y_side, y_side]
        return call(
            functools.partial(update_kernel, elems=elems, n_elem=n_elem, slot=slot, last=last),
            name,
            (u, k, *x_halo, *tables, *squares, carry),
            out,
            (
                pltpu.VMEM((comps, 2, rows, size_z), f32),
                pltpu.VMEM((comps, 2, rows, size_z), f32),
                pltpu.VMEM((8, 2, rows, size_z), f32),
                pltpu.VMEM((5, 2, rows, size_z), f32),
                pltpu.VMEM((5, 2, rows, size_z), f32),
                pltpu.VMEM((5, 2, NODES, LANES), f32),
            ),
            us=2.0,
        )

    def halos(v, y_rows):
        y_halo = swap(*y_rows, "gy")
        sides = call(faces_kernel, "faces", (*v, *y_halo), (x_side, x_side), us=0.3)
        return y_halo, swap(*sides, "gx")

    def step(v, y_rows, carry, slot):
        y_halo, x_halo = halos(v, y_rows)
        u_mid, k_mid, sq_mid = main(v, (), mid, "middle")
        u_edge, k_edge, sq_edge = main(v, y_halo, edge, "edges")
        k_edge, f_edge, carry, *y_rows = update(
            u_edge, k_edge, x_halo, (sq_mid, sq_edge), carry, edge, slot, "update_edges"
        )
        k_mid, f_mid, carry = update(
            u_mid, k_mid, x_halo, (), carry, mid, slot, "update_middle"
        )
        return (k_mid, k_edge), (u_mid, u_edge, f_mid, f_edge), y_rows, carry

    y_rows = call(rows_kernel, "rows", (rhs_loads,), (y_side, y_side), us=0.1)
    carry = jnp.zeros((4, NODES, LANES), f32)
    k_loads, loads, y_rows, carry = step((rhs_loads, rhs_loads), y_rows, carry, 0)
    k_image, image, y_rows, sums = step(k_loads, y_rows, carry, 1)
    y_halo, x_halo = halos(k_image, y_rows)
    sums = lax.all_to_all(sums, axes, 0, 0, tiled=True)
    return tuple(
        call(
            finish_kernel,
            "finish",
            (*k_image, *y_halo, *x_halo, free, *loads, *image, sums),
            (shape(*rhs_loads.shape),) * 2,
            (
                pltpu.VMEM((size_x, comps, size_y, size_z), f32),
                pltpu.VMEM((size_x, comps, size_y, size_z), f32),
                pltpu.SemaphoreType.DMA((2, size_x)),
            ),
            us=4.0,
            out_spec=pl.BlockSpec(memory_space=pltpu.HBM),
        )
    )


def solution(mesh):
    in_specs = (P(None, "gx", "gy", None), P("gx", "gy", None), P("gx", "gy"))
    out_specs = (P(None, "gx", "gy", None), P(None, "gx", "gy", None))
    return jax.shard_map(local, mesh=mesh, in_specs=in_specs, out_specs=out_specs, check_vma=False)
```

```python
import functools

import jax
import jax.numpy as jnp
import numpy as np
from jax import lax
from jax.experimental import pallas as pl
from jax.experimental.pallas import tpu as pltpu
from jax.sharding import PartitionSpec as P

ORDER = 7
NODES = ORDER + 1
LANES = 128

POISSON = 0.3
LAME_FIRST = POISSON / ((1.0 + POISSON) * (1.0 - 2.0 * POISSON))
LAME_SHEAR = 1.0 / (2.0 * (1.0 + POISSON))
SOLID_MODULUS = 0.1
VOID_MODULUS = 0.001
INTERIOR_POINTS = (
    -0.8717401485096066,
    -0.5917001814331423,
    -0.2092992179024789,
    0.2092992179024789,
    0.5917001814331423,
    0.8717401485096066,
)
VMEM_LIMIT = 10 * 1024 * 1024


def legendre_value(poly_order, point):
    previous = 1.0
    current = point
    for degree in range(1, poly_order):
        following = ((2.0 * degree + 1.0) * point * current - degree * previous) / (degree + 1.0)
        previous = current
        current = following
    return current


def gll_tables(poly_order):
    points = np.array([-1.0] + list(INTERIOR_POINTS) + [1.0])
    values = np.array([legendre_value(poly_order, float(point)) for point in points])
    weights = 2.0 / (poly_order * (poly_order + 1) * values**2)
    node_count = poly_order + 1
    derivative = np.zeros((node_count, node_count))
    for row_index in range(node_count):
        for col_index in range(node_count):
            if row_index != col_index:
                derivative[row_index, col_index] = values[row_index] / (
                    values[col_index] * (points[row_index] - points[col_index])
                )
    derivative[0, 0] = -poly_order * (poly_order + 1) / 4.0
    derivative[poly_order, poly_order] = poly_order * (poly_order + 1) / 4.0
    return (derivative, weights)


DERIV, WEIGHTS = gll_tables(ORDER)
HALF = NODES // 2
ODD = [[0.5 * (DERIV[a, i] - DERIV[a, ORDER - i]) for i in range(HALF)] for a in range(HALF)]
EVEN = [[0.5 * (DERIV[a, i] + DERIV[a, ORDER - i]) for i in range(HALF)] for a in range(HALF)]


def z_table(matrix):
    blocks = np.kron(np.eye(LANES // NODES), matrix).astype(np.float32)
    high = blocks.astype(jnp.bfloat16)
    low = (blocks - high.astype(np.float32)).astype(jnp.bfloat16)
    row = np.concatenate([high, low], axis=1)
    return np.concatenate([row, row], axis=0)


def shared_halves(local_len, offset, global_len, node_count):
    position = jnp.arange(local_len, dtype=jnp.int32)
    node_index = position % node_count
    global_pos = position + offset
    shared = (node_index == 0) & (global_pos > 0) | (node_index == node_count - 1) & (
        global_pos < global_len - 1
    )
    return jnp.where(shared, 0.5, 1.0).astype(jnp.float32)


def combine(coefs, terms):
    total = None
    for coef, term in zip(coefs, terms):
        part = float(coef) * term
        total = part if total is None else total + part
    return total


def parts(n_elem):
    return tuple(range(1, n_elem - 1)), (0, n_elem - 1)


def locate(refs, elem, n_elem):
    if refs[0].shape[2] == n_elem * NODES:
        return refs[0], elem * NODES
    for ref, group in zip(refs, parts(n_elem)):
        if elem in group:
            return ref, group.index(elem) * NODES


def row_sum_y(refs, lo, hi, comp, plane, elem, n_elem):
    ref, base = locate(refs, elem, n_elem)
    own = ref[comp, plane, base : base + NODES, :]
    if elem > 0:
        ref, base = locate(refs, elem - 1, n_elem)
        lo = ref[comp, plane, base + ORDER : base + NODES, :]
    if elem < n_elem - 1:
        ref, base = locate(refs, elem + 1, n_elem)
        hi = ref[comp, plane, base : base + 1, :]
    sub = lax.broadcasted_iota(jnp.int32, own.shape, 0)
    lo = jnp.broadcast_to(lo, own.shape)
    hi = jnp.broadcast_to(hi, own.shape)
    return own + jnp.where(sub == 0, lo, jnp.where(sub == ORDER, hi, 0.0))


def sum_z(rows):
    size = rows.shape[-1]
    lane = lax.broadcasted_iota(jnp.int32, rows.shape, 1)
    ahead = pltpu.roll(rows, size - 1, 1)
    behind = pltpu.roll(rows, 1, 1)
    upper = (lane % NODES == ORDER) & (lane < size - 1)
    lower = (lane % NODES == 0) & (lane > 0)
    return rows + jnp.where(upper, ahead, jnp.where(lower, behind, 0.0))


def release(rows, free):
    return jnp.concatenate([rows[:, :LANES] * free, rows[:, LANES:]], axis=1)


def fold(strip):
    total = strip[:, :LANES]
    for start in range(LANES, strip.shape[1], LANES):
        total = total + strip[:, start : start + LANES]
    return total


def is_upper(axis):
    return lax.axis_index(axis) % 2


def pick(upper, near, far):
    mask = jnp.full(near.shape, upper, jnp.int32) == 1
    return jnp.where(mask, near, far), jnp.where(mask, far, near)


def y_sides(upper, near_ref, far_ref, comp, plane):
    row = slice(plane, plane + 1)
    return pick(upper, near_ref[comp, row, :], far_ref[comp, row, :])


def x_side(upper, near_ref, far_ref, comp, elem, n_elem, end):
    rows = side_rows(comp, elem, n_elem)
    return pick(upper, near_ref[rows, :], far_ref[rows, :])[end]


def columns(y_col_ref, which):
    return [y_col_ref[which, j] for j in range(NODES)]


def column_sum(cols, row_of):
    total = None
    for j in range(NODES):
        part = cols[j] * jnp.broadcast_to(row_of(j), (NODES, LANES))
        total = part if total is None else total + part
    return total


def along_z(flat, table):
    high = flat.astype(jnp.bfloat16)
    low = (flat - high.astype(jnp.float32)).astype(jnp.bfloat16)
    both = jnp.dot(
        jnp.concatenate([high, low], axis=1), table, preferred_element_type=jnp.float32
    )
    return both[:, :LANES] + both[:, LANES:]


def main_kernel(*refs, elems, n_elem):
    v_refs, refs = refs[:2], refs[2:]
    if 0 in elems:
        ynear_ref, yfar_ref = refs[:2]
        refs = refs[2:]
    free_ref, elem_ref, half_ref, halfz_ref, zmat_ref, ycol_ref = refs[:6]
    u_ref, k_ref, square_ref = refs[6:9]
    grad_ref, stress_ref, side_ref, along_ref = refs[9:]
    comps, planes, size_y, size_z = u_ref.shape
    n_tile = size_z // LANES
    y_upper = is_upper("gy")
    square = jnp.zeros((NODES, LANES), jnp.float32)
    for place, elem in enumerate(elems):
        base = elem * NODES
        sub = slice(place * NODES, (place + 1) * NODES)
        for plane in range(planes):
            part = None
            for comp in range(comps):
                lo = hi = None
                if elem in (0, n_elem - 1):
                    lo, hi = y_sides(y_upper, ynear_ref, yfar_ref, comp, plane)
                strip = sum_z(row_sum_y(v_refs, lo, hi, comp, plane, elem, n_elem))
                strip = release(strip, free_ref[plane, base : base + NODES, :])
                u_ref[comp, plane, sub, :] = strip
                part = strip * strip if part is None else part + strip * strip
            if plane not in (0, ORDER):
                part = fold(part * halfz_ref[0:1, :])
                square = square + part * half_ref[plane, base : base + NODES, :]
    square_ref[...] = square

    rows = comps * planes * size_y
    for tile in range(n_tile):
        lanes = slice(tile * LANES, (tile + 1) * LANES)
        flat = u_ref[:, :, :, lanes].reshape(rows, LANES)
        grad_ref[:, :, :, lanes] = along_z(flat, zmat_ref[0]).reshape(
            comps, planes, size_y, LANES
        )

    def block(tile, place):
        lanes = pl.ds(pl.multiple_of(tile * LANES, LANES), LANES)
        base = place * NODES
        sub = slice(base, base + NODES)
        cols = columns(ycol_ref, 0)
        for c in range(3):
            for plane in range(NODES):
                along_ref[c, plane] = column_sum(
                    cols, lambda j: u_ref[c, plane, base + j : base + j + 1, lanes]
                )
        even, odd = [], []
        for comp in range(3):
            vals = [u_ref[comp, i, sub, lanes] for i in range(NODES)]
            even.append([vals[i] + vals[ORDER - i] for i in range(HALF)])
            odd.append([vals[i] - vals[ORDER - i] for i in range(HALF)])
        scale = elem_ref[elems[place] * NODES : (elems[place] + 1) * NODES, lanes]
        xsum = [[None] * HALF for _ in range(3)]
        xdif = [[None] * HALF for _ in range(3)]
        for pair in range(HALF):
            first = [combine(ODD[pair], odd[c]) for c in range(3)]
            second = [combine(EVEN[pair], even[c]) for c in range(3)]
            side_x = []
            for plane, sign in ((pair, 1), (ORDER - pair, -1)):
                gx = [first[c] + second[c] if sign > 0 else first[c] - second[c] for c in range(3)]
                gy = [along_ref[c, plane] for c in range(3)]
                gz = [grad_ref[c, plane, sub, lanes] for c in range(3)]
                shear = scale * float(LAME_SHEAR * WEIGHTS[plane])
                twice = scale * float(2.0 * LAME_SHEAR * WEIGHTS[plane])
                spread = (gx[0] + gy[1] + gz[2]) * (scale * float(LAME_FIRST * WEIGHTS[plane]))
                sxx = twice * gx[0] + spread
                syy = twice * gy[1] + spread
                szz = twice * gz[2] + spread
                sxy = shear * (gx[1] + gy[0])
                sxz = shear * (gx[2] + gz[0])
                syz = shear * (gy[2] + gz[1])
                side_x.append((sxx, sxy, sxz))
                for c, value in enumerate((sxz, syz, szz)):
                    stress_ref[c, plane, sub, lanes] = value
                for c, value in enumerate((sxy, syy, syz)):
                    side_ref[c, plane, :, :] = value
            for c in range(3):
                se = side_x[0][c] + side_x[1][c]
                so = side_x[0][c] - side_x[1][c]
                for i in range(HALF):
                    add_x = float(EVEN[pair][i]) * so
                    add_y = float(ODD[pair][i]) * se
                    xsum[c][i] = add_x if pair == 0 else xsum[c][i] + add_x
                    xdif[c][i] = add_y if pair == 0 else xdif[c][i] + add_y
        cols = columns(ycol_ref, 1)
        for c in range(3):
            for plane in range(NODES):
                i = min(plane, ORDER - plane)
                total = xsum[c][i] + xdif[c][i] if plane < HALF else xsum[c][i] - xdif[c][i]
                k_ref[c, plane, sub, lanes] = total + column_sum(
                    cols, lambda b: side_ref[c, plane, b : b + 1, :]
                )

    @pl.loop(0, n_tile)
    def _(tile):
        for place in range(len(elems)):
            block(tile, place)

    for tile in range(n_tile):
        lanes = slice(tile * LANES, (tile + 1) * LANES)
        flat = stress_ref[:, :, :, lanes].reshape(rows, LANES)
        k_ref[:, :, :, lanes] += along_z(flat, zmat_ref[1]).reshape(comps, planes, size_y, LANES)


SHEAR, FIRST = float(LAME_SHEAR), float(LAME_FIRST)
DIAG = 2.0 * SHEAR + FIRST
ENDS = (0, ORDER)
THROUGH = np.einsum("ai,a,ap->ip", DERIV, WEIGHTS, DERIV)
ONWARD = DERIV.T
BACKWARD = WEIGHTS[:, None] * DERIV


def spread_pair(total_p, total_m, table, i, sign, even, odd):
    alpha = 0.5 * float(table[i, 0] + table[i, ORDER]) * even
    beta = 0.5 * float(table[i, 0] - table[i, ORDER]) * odd
    plus, minus = (alpha, beta) if sign > 0 else (beta, alpha)
    if total_p is None:
        return plus, minus
    return total_p + plus, total_m + minus


def update_kernel(*refs, elems, n_elem, slot, last):
    u_ref, kin_ref, xnear_ref, xfar_ref = refs[:4]
    free_ref, elem_ref, half_ref, halfz_ref, zmat_ref, ycol_ref = refs[4:10]
    squares_refs, refs = (refs[10:12], refs[12:]) if 0 in elems else ((), refs[10:])
    carry_ref, k_ref, face_ref, sums_ref = refs[:4]
    refs = refs[4:]
    if 0 in elems:
        near_ref, far_ref = refs[:2]
        refs = refs[2:]
    add_ref, grad_ref, keep_ref, zin_ref, zout_ref, side_ref = refs
    comps, planes, size_y, size_z = k_ref.shape
    n_tile = size_z // LANES
    x_upper = is_upper("gx")
    square = jnp.zeros((NODES, LANES), jnp.float32)
    for ref in squares_refs:
        square = square + ref[...]
    for place, elem in enumerate(elems):
        rows = slice(elem * NODES, (elem + 1) * NODES)
        own = slice(place * NODES, (place + 1) * NODES)
        for end, plane in enumerate(ENDS):
            part = None
            for comp in range(comps):
                strip = x_side(x_upper, xnear_ref, xfar_ref, comp, elem, n_elem, end)
                strip = release(sum_z(strip), free_ref[plane, rows, :])
                add_ref[comp, end, own, :] = strip
                strip = strip + u_ref[comp, plane, own, :]
                face_ref[comp, end, own, :] = strip
                part = strip * strip if part is None else part + strip * strip
            square = square + fold(part * halfz_ref[0:1, :]) * half_ref[plane, rows, :]

    for tile in range(n_tile):
        lanes = slice(tile * LANES, (tile + 1) * LANES)
        flat = add_ref[:, :, :, lanes].reshape(comps * 2 * size_y, LANES)
        grad_ref[:, :, :, lanes] = along_z(flat, zmat_ref[0]).reshape(comps, 2, size_y, LANES)

    @pl.loop(0, n_tile)
    def _(tile):
        lanes = pl.ds(pl.multiple_of(tile * LANES, LANES), LANES)
        for place, elem in enumerate(elems):
            base = place * NODES
            sub = slice(base, base + NODES)
            scale = elem_ref[elem * NODES : (elem + 1) * NODES, lanes]
            cols = columns(ycol_ref, 0)
            for end, plane in enumerate(ENDS):
                gy = [
                    column_sum(
                        cols, lambda j: add_ref[c, end, base + j : base + j + 1, lanes]
                    )
                    for c in range(3)
                ]
                gz = [grad_ref[c, end, sub, lanes] for c in range(3)]
                own = scale * float(WEIGHTS[plane])
                axx = own * (FIRST * (gy[1] + gz[2]))
                axy = own * (SHEAR * gy[0])
                axz = own * (SHEAR * gz[0])
                ayy = own * (DIAG * gy[1] + FIRST * gz[2])
                azz = own * (DIAG * gz[2] + FIRST * gy[1])
                ayz = own * (SHEAR * (gy[2] + gz[1]))
                scaled = [scale * add_ref[c, end, sub, lanes] for c in range(3)]
                for c, value in enumerate((SHEAR * scaled[2], FIRST * scaled[0], axz, ayz, azz)):
                    zin_ref[c, end, sub, lanes] = value
                for c, value in enumerate((SHEAR * scaled[1], FIRST * scaled[0], axy, ayy, ayz)):
                    side_ref[c, end, :, :] = value
                for c, value in enumerate((axx, axy, axz)):
                    keep_ref[c, end, sub, lanes] = value
            cols = columns(ycol_ref, 1)
            for end in range(2):
                for c in range(5):
                    keep_ref[3 + c, end, sub, lanes] = column_sum(
                        cols, lambda b: side_ref[c, end, b : b + 1, :]
                    )

    for tile in range(n_tile):
        lanes = slice(tile * LANES, (tile + 1) * LANES)
        flat = zin_ref[:, :, :, lanes].reshape(5 * 2 * size_y, LANES)
        zout_ref[:, :, :, lanes] = along_z(flat, zmat_ref[1]).reshape(5, 2, size_y, LANES)

    def tile_energy(tile, energy):
        lanes = pl.ds(pl.multiple_of(tile * LANES, LANES), LANES)
        for place, elem in enumerate(elems):
            sub = slice(place * NODES, (place + 1) * NODES)
            scale = elem_ref[elem * NODES : (elem + 1) * NODES, lanes]
            zout = [[zout_ref[c, end, sub, lanes] for end in range(2)] for c in range(5)]
            kept = [[keep_ref[c, end, sub, lanes] for end in range(2)] for c in range(8)]
            back = (
                [kept[3][end] + zout[0][end] for end in range(2)],
                kept[4],
                zout[1],
            )
            for c in range(3):
                factor = scale * (DIAG if c == 0 else SHEAR)
                pairs = (
                    ([factor * add_ref[c, end, sub, lanes] for end in range(2)], THROUGH, 1),
                    (kept[c], ONWARD, -1),
                    (back[c], BACKWARD, -1),
                )
                pairs = [(v[0] + v[1], v[0] - v[1], table, sign) for v, table, sign in pairs]
                for i in range(HALF):
                    plus = minus = None
                    for even, odd, table, sign in pairs:
                        plus, minus = spread_pair(plus, minus, table, i, sign, even, odd)
                    for plane, value in ((i, plus + minus), (ORDER - i, plus - minus)):
                        value = value + kin_ref[c, plane, sub, lanes]
                        if plane in ENDS:
                            end = ENDS.index(plane)
                            value = value + (kept[5 + c][end] + zout[2 + c][end])
                            vector = face_ref[c, end, sub, lanes]
                        else:
                            vector = u_ref[c, plane, sub, lanes]
                        k_ref[c, plane, sub, lanes] = value
                        energy = energy + value * vector
        return energy

    energy = lax.fori_loop(0, n_tile, tile_energy, jnp.zeros((NODES, LANES), jnp.float32))
    if 0 in elems:
        put_rows(
            lambda comp, plane: k_ref[comp, plane, 0:1, :],
            lambda comp, plane: k_ref[comp, plane, size_y - 1 : size_y, :],
            near_ref,
            far_ref,
        )
    moments = [carry_ref[i] for i in range(4)]
    moments[2 * slot] = moments[2 * slot] + square
    moments[2 * slot + 1] = moments[2 * slot + 1] + energy
    if not last:
        for i in range(4):
            sums_ref[i] = moments[i]
    else:
        lane = lax.broadcasted_iota(jnp.int32, sums_ref.shape, 1)
        known = jnp.zeros(sums_ref.shape, jnp.float32)
        for i in range(4):
            known = jnp.where(lane == i, jnp.sum(moments[i]), known)
        sums_ref[...] = known


def put_rows(lo_of, hi_of, near_ref, far_ref):
    y_upper = is_upper("gy")
    comps, planes, _ = near_ref.shape
    for comp in range(comps):
        for plane in range(planes):
            row = slice(plane, plane + 1)
            far_ref[comp, row, :], near_ref[comp, row, :] = pick(
                y_upper, hi_of(comp, plane), lo_of(comp, plane)
            )


def scale_kernel(flags_ref, widen_ref, weight_ref, scale_ref):
    solid = (flags_ref[...] == 1).astype(jnp.bfloat16)
    solid = jnp.dot(solid, widen_ref[...], preferred_element_type=jnp.float32)
    modulus = jnp.where(solid > 0.5, SOLID_MODULUS, VOID_MODULUS).astype(jnp.float32)
    for elem in range(flags_ref.shape[0]):
        scale_ref[elem * NODES : (elem + 1) * NODES, :] = (
            modulus[elem : elem + 1, :] * weight_ref[...]
        )


def rows_kernel(v_ref, near_ref, far_ref):
    size_y = v_ref.shape[2]
    put_rows(
        lambda comp, plane: v_ref[comp, plane, 0:1, :],
        lambda comp, plane: v_ref[comp, plane, size_y - 1 : size_y, :],
        near_ref,
        far_ref,
    )


def side_rows(comp, elem, n_elem):
    start = comp * (n_elem * ORDER + 1) + elem * ORDER
    return slice(start, start + NODES)


def faces_kernel(*refs, n_elem):
    vmid_ref, vedge_ref, ynear_ref, yfar_ref = refs[:4]
    near_ref, far_ref = refs[-2:]
    comps = vmid_ref.shape[0]
    x_upper, y_upper = is_upper("gx"), is_upper("gy")
    v_refs = vmid_ref, vedge_ref
    for comp in range(comps):
        sides = [y_sides(y_upper, ynear_ref, yfar_ref, comp, plane) for plane in ENDS]
        for elem in range(n_elem):
            rows = side_rows(comp, elem, n_elem)
            lo, hi = [
                row_sum_y(v_refs, *side, comp, plane, elem, n_elem)
                for plane, side in zip(ENDS, sides)
            ]
            near_ref[rows, :], far_ref[rows, :] = pick(x_upper, lo, hi)


def assemble_kernel(kmid_ref, kedge_ref, free_ref, w_ref, done_ref, *, elems, n_elem):
    for place, elem in enumerate(elems):
        own = slice(place * NODES, (place + 1) * NODES)
        sub = slice(elem * NODES, (elem + 1) * NODES)
        for plane in range(w_ref.shape[1]):
            for comp in range(w_ref.shape[0]):
                rows = row_sum_y((kmid_ref, kedge_ref), None, None, comp, plane, elem, n_elem)
                w_ref[comp, plane, own, :] = release(sum_z(rows), free_ref[plane, sub, :])
    done_ref[...] = w_ref[0, 0, 0:NODES, :LANES]


def finish_kernel(*refs):
    *k_refs, w_ref = refs[:3]
    ynear_ref, yfar_ref, xnear_ref, xfar_ref, free_ref = refs[3:8]
    r_refs, r_faces, q_refs, q_faces = refs[8:10], refs[10:12], refs[12:14], refs[14:16]
    sums_ref, adj_out, res_out, adj_ref, res_ref, sem_ref = refs[16:]
    planes, comps, size_y, _ = adj_ref.shape
    n_elem = size_y // NODES
    x_upper, y_upper = is_upper("gx"), is_upper("gy")
    sums = jnp.sum(sums_ref[...], axis=0, keepdims=True)
    lane = lax.broadcasted_iota(jnp.int32, sums.shape, 1)
    m0, m1, m2, m3 = [
        jnp.sum(jnp.where(lane == i, sums, 0.0), axis=1, keepdims=True) for i in range(4)
    ]
    first = m0 / m1
    following = first * first * m2 - m0
    ratio = following / m0
    grow = 1.0 + ratio
    second = following / (grow * grow * m1 - 2.0 * first * grow * m2 + first * first * m3)
    lead = first + second * grow
    cross = first * second
    copies = []
    for plane in range(planes):
        end = ENDS.index(plane) if plane in ENDS else None
        place = plane if end is None else end
        for comp in range(comps):
            for elem in range(n_elem):
                sub = slice(elem * NODES, (elem + 1) * NODES)
                r_ref, row = locate(r_refs if end is None else r_faces, elem, n_elem)
                q_ref, row = locate(q_refs if end is None else q_faces, elem, n_elem)
                own = slice(row, row + NODES)
                strip = None
                if end is not None:
                    strip = x_side(x_upper, xnear_ref, xfar_ref, comp, elem, n_elem, end)
                if elem in (0, n_elem - 1):
                    lo, hi = y_sides(y_upper, ynear_ref, yfar_ref, comp, plane)
                    rows = row_sum_y(k_refs, lo, hi, comp, plane, elem, n_elem)
                    strip = rows if strip is None else strip + rows
                if strip is not None:
                    strip = release(sum_z(strip), free_ref[plane, sub, :])
                if elem not in (0, n_elem - 1):
                    rows = w_ref[comp, plane, own, :]
                    strip = rows if strip is None else strip + rows
                loads = r_ref[comp, place, own, :]
                image = q_ref[comp, place, own, :]
                adj_ref[plane, comp, sub, :] = lead * loads - cross * image
                res_ref[plane, comp, sub, :] = loads - lead * image + cross * strip
        for which, (ref, out) in enumerate(((adj_ref, adj_out), (res_ref, res_out))):
            copy = pltpu.make_async_copy(ref.at[plane], out.at[:, plane], sem_ref.at[which, plane])
            copy.start()
            copies.append(copy)
    for copy in copies:
        copy.wait()


def swap(near_out, far_out, axis):
    count = lax.axis_size(axis)
    inner = [(i, i ^ 1) for i in range(count)]
    outer = [(i, ((i + 1) ^ 1) - 1) for i in range(1, count - 1)]
    far = lax.ppermute(far_out, axis, outer)
    near = lax.ppermute(near_out, axis, inner)
    return near, far


def local(rhs_loads, flags, fixed):
    comps, size_x, size_y, size_z = rhs_loads.shape
    axes = ("gx", "gy")
    devices = lax.axis_size("gx") * lax.axis_size("gy")
    f32 = jnp.float32
    y_side = jax.ShapeDtypeStruct((comps, size_x, size_z), f32)
    side_len = comps * (size_y // NODES * ORDER + 1)
    side = jax.ShapeDtypeStruct((side_len + -side_len % NODES, size_z), f32)
    whole = pl.BlockSpec(memory_space=pltpu.VMEM)

    n_elem, n_deep = flags.shape[1:]
    widen = jnp.asarray(np.kron(np.eye(n_deep), np.ones((1, NODES))), jnp.bfloat16)
    weight_yz = jnp.asarray(WEIGHTS[:, None] * np.tile(WEIGHTS, n_deep)[None, :], f32)
    elem_scale = pl.pallas_call(
        scale_kernel,
        in_specs=[whole] * 3,
        out_specs=whole,
        out_shape=jax.ShapeDtypeStruct((size_y, size_z), f32),
        compiler_params=pltpu.CompilerParams(vmem_limit_bytes=VMEM_LIMIT),
        cost_estimate=pl.CostEstimate(flops=1000, bytes_accessed=100000, transcendentals=0),
        name="scale",
    )(flags[0], widen, weight_yz)
    free = 1.0 - fixed.astype(f32)[:, :, None] * (jnp.arange(LANES) == 0).astype(f32)
    half_xy = (
        shared_halves(size_x, lax.axis_index("gx") * size_x, size_x * lax.axis_size("gx"), NODES)[
            :, None, None
        ]
        * shared_halves(
            size_y, lax.axis_index("gy") * size_y, size_y * lax.axis_size("gy"), NODES
        )[None, :, None]
        * jnp.ones((LANES,), f32)
    )
    half_z = jnp.broadcast_to(shared_halves(size_z, 0, size_z, NODES)[None], (NODES, size_z))
    z_mat = jnp.asarray(np.stack([z_table(DERIV.T), z_table(DERIV)]))
    y_col = jnp.asarray(
        np.broadcast_to(
            np.stack([DERIV.T, DERIV])[:, :, :, None], (2, NODES, NODES, LANES)
        ),
        f32,
    )

    mid, edge = parts(n_elem)
    tables = (free, elem_scale, half_xy, half_z, z_mat, y_col)

    def shape(*sizes):
        return jax.ShapeDtypeStruct(sizes, f32)

    def call(
        kernel, name, args, out_shape, scratch=(), us=1.0, out_spec=whole
    ):
        return pl.pallas_call(
            kernel,
            in_specs=[whole] * len(args),
            out_specs=[out_spec] * len(out_shape),
            out_shape=list(out_shape),
            scratch_shapes=list(scratch),
            compiler_params=pltpu.CompilerParams(vmem_limit_bytes=VMEM_LIMIT),
            cost_estimate=pl.CostEstimate(
                flops=int(us * 4e6), bytes_accessed=int(us * 2.5e6), transcendentals=0
            ),
            name=name,
        )(*args)

    def main(v, y_halo, elems, name):
        some = (comps, size_x, len(elems) * NODES, size_z)
        return call(
            functools.partial(main_kernel, elems=elems, n_elem=n_elem),
            name,
            (*v, *y_halo, *tables),
            (shape(*some), shape(*some), shape(NODES, LANES)),
            (
                pltpu.VMEM(some, f32),
                pltpu.VMEM(some, f32),
                pltpu.VMEM((comps, size_x, NODES, LANES), f32),
                pltpu.VMEM((comps, size_x, NODES, LANES), f32),
            ),
            us=5.0,
        )

    def update(u, k, x_halo, squares, carry, elems, slot, name):
        rows = len(elems) * NODES
        last = slot == 1 and 0 not in elems
        out = [
            shape(comps, size_x, rows, size_z),
            shape(comps, 2, rows, size_z),
            shape(devices, LANES) if last else shape(4, NODES, LANES),
        ]
        if 0 in elems:
            out += [y_side, y_side]
        return call(
            functools.partial(update_kernel, elems=elems, n_elem=n_elem, slot=slot, last=last),
            name,
            (u, k, *x_halo, *tables, *squares, carry),
            out,
            (
                pltpu.VMEM((comps, 2, rows, size_z), f32),
                pltpu.VMEM((comps, 2, rows, size_z), f32),
                pltpu.VMEM((8, 2, rows, size_z), f32),
                pltpu.VMEM((5, 2, rows, size_z), f32),
                pltpu.VMEM((5, 2, rows, size_z), f32),
                pltpu.VMEM((5, 2, NODES, LANES), f32),
            ),
            us=2.0,
        )

    def y_halos(y_rows):
        return swap(*y_rows, "gy")

    def x_halos(v, y_halo, after):
        sides = call(
            functools.partial(faces_kernel, n_elem=n_elem),
            "faces",
            (*v, *y_halo, *after),
            (side, side),
            us=0.3,
        )
        return swap(*sides, "gx")

    def step(v, y_rows, carry, slot):
        y_halo = y_halos(y_rows)
        u_mid, k_mid, sq_mid = main(v, (), mid, "middle")
        x_halo = x_halos(v, y_halo, ())
        u_edge, k_edge, sq_edge = main(v, y_halo, edge, "edges")
        k_edge, f_edge, carry, *y_rows = update(
            u_edge, k_edge, x_halo, (sq_mid, sq_edge), carry, edge, slot, "update_edges"
        )
        k_mid, f_mid, carry = update(
            u_mid, k_mid, x_halo, (), carry, mid, slot, "update_middle"
        )
        return (k_mid, k_edge), (u_mid, u_edge, f_mid, f_edge), y_rows, carry

    y_rows = call(rows_kernel, "rows", (rhs_loads,), (y_side, y_side), us=0.1)
    carry = jnp.zeros((4, NODES, LANES), f32)
    k_loads, loads, y_rows, carry = step((rhs_loads, rhs_loads), y_rows, carry, 0)
    k_image, image, y_rows, sums = step(k_loads, y_rows, carry, 1)
    y_halo = y_halos(y_rows)
    w_mid, done = call(
        functools.partial(assemble_kernel, elems=mid, n_elem=n_elem),
        "assemble",
        (*k_image, free),
        (shape(comps, size_x, len(mid) * NODES, size_z), shape(NODES, LANES)),
        us=1.0,
    )
    x_halo = x_halos(k_image, y_halo, (done,))
    sums = lax.all_to_all(sums, axes, 0, 0, tiled=True)
    return tuple(
        call(
            finish_kernel,
            "finish",
            (*k_image, w_mid, *y_halo, *x_halo, free, *loads, *image, sums),
            (shape(*rhs_loads.shape),) * 2,
            (
                pltpu.VMEM((size_x, comps, size_y, size_z), f32),
                pltpu.VMEM((size_x, comps, size_y, size_z), f32),
                pltpu.SemaphoreType.DMA((2, size_x)),
            ),
            us=4.0,
            out_spec=pl.BlockSpec(memory_space=pltpu.HBM),
        )
    )


def solution(mesh):
    in_specs = (P(None, "gx", "gy", None), P("gx", "gy", None), P("gx", "gy"))
    out_specs = (P(None, "gx", "gy", None), P(None, "gx", "gy", None))
    return jax.shard_map(local, mesh=mesh, in_specs=in_specs, out_specs=out_specs, check_vma=False)
```

```python
import functools

import jax
import jax.numpy as jnp
import numpy as np
from jax import lax
from jax.experimental import pallas as pl
from jax.experimental.pallas import tpu as pltpu
from jax.sharding import PartitionSpec as P

ORDER = 7
NODES = ORDER + 1
LANES = 128

POISSON = 0.3
LAME_FIRST = POISSON / ((1.0 + POISSON) * (1.0 - 2.0 * POISSON))
LAME_SHEAR = 1.0 / (2.0 * (1.0 + POISSON))
SOLID_MODULUS = 0.1
VOID_MODULUS = 0.001
INTERIOR_POINTS = (
    -0.8717401485096066,
    -0.5917001814331423,
    -0.2092992179024789,
    0.2092992179024789,
    0.5917001814331423,
    0.8717401485096066,
)
VMEM_LIMIT = 10 * 1024 * 1024


def legendre_value(poly_order, point):
    previous = 1.0
    current = point
    for degree in range(1, poly_order):
        following = ((2.0 * degree + 1.0) * point * current - degree * previous) / (degree + 1.0)
        previous = current
        current = following
    return current


def gll_tables(poly_order):
    points = np.array([-1.0] + list(INTERIOR_POINTS) + [1.0])
    values = np.array([legendre_value(poly_order, float(point)) for point in points])
    weights = 2.0 / (poly_order * (poly_order + 1) * values**2)
    node_count = poly_order + 1
    derivative = np.zeros((node_count, node_count))
    for row_index in range(node_count):
        for col_index in range(node_count):
            if row_index != col_index:
                derivative[row_index, col_index] = values[row_index] / (
                    values[col_index] * (points[row_index] - points[col_index])
                )
    derivative[0, 0] = -poly_order * (poly_order + 1) / 4.0
    derivative[poly_order, poly_order] = poly_order * (poly_order + 1) / 4.0
    return (derivative, weights)


DERIV, WEIGHTS = gll_tables(ORDER)
HALF = NODES // 2
ODD = [[0.5 * (DERIV[a, i] - DERIV[a, ORDER - i]) for i in range(HALF)] for a in range(HALF)]
EVEN = [[0.5 * (DERIV[a, i] + DERIV[a, ORDER - i]) for i in range(HALF)] for a in range(HALF)]


def z_table(matrix):
    blocks = np.kron(np.eye(LANES // NODES), matrix).astype(np.float32)
    high = blocks.astype(jnp.bfloat16)
    low = (blocks - high.astype(np.float32)).astype(jnp.bfloat16)
    row = np.concatenate([high, low], axis=1)
    return np.concatenate([row, row], axis=0)


def shared_halves(local_len, offset, global_len, node_count):
    position = jnp.arange(local_len, dtype=jnp.int32)
    node_index = position % node_count
    global_pos = position + offset
    shared = (node_index == 0) & (global_pos > 0) | (node_index == node_count - 1) & (
        global_pos < global_len - 1
    )
    return jnp.where(shared, 0.5, 1.0).astype(jnp.float32)


def combine(coefs, terms):
    total = None
    for coef, term in zip(coefs, terms):
        part = float(coef) * term
        total = part if total is None else total + part
    return total


def parts(n_elem):
    return tuple(range(1, n_elem - 1)), (0, n_elem - 1)


def locate(refs, elem, n_elem):
    if refs[0].shape[2] == n_elem * NODES:
        return refs[0], elem * NODES
    for ref, group in zip(refs, parts(n_elem)):
        if elem in group:
            return ref, group.index(elem) * NODES


def row_sum_y(refs, lo, hi, comp, plane, elem, n_elem):
    ref, base = locate(refs, elem, n_elem)
    own = ref[comp, plane, base : base + NODES, :]
    if elem > 0:
        ref, base = locate(refs, elem - 1, n_elem)
        lo = ref[comp, plane, base + ORDER : base + NODES, :]
    if elem < n_elem - 1:
        ref, base = locate(refs, elem + 1, n_elem)
        hi = ref[comp, plane, base : base + 1, :]
    sub = lax.broadcasted_iota(jnp.int32, own.shape, 0)
    lo = jnp.broadcast_to(lo, own.shape)
    hi = jnp.broadcast_to(hi, own.shape)
    return own + jnp.where(sub == 0, lo, jnp.where(sub == ORDER, hi, 0.0))


def sum_z(rows):
    size = rows.shape[-1]
    lane = lax.broadcasted_iota(jnp.int32, rows.shape, 1)
    ahead = pltpu.roll(rows, size - 1, 1)
    behind = pltpu.roll(rows, 1, 1)
    upper = (lane % NODES == ORDER) & (lane < size - 1)
    lower = (lane % NODES == 0) & (lane > 0)
    return rows + jnp.where(upper, ahead, jnp.where(lower, behind, 0.0))


def release(rows, free):
    return jnp.concatenate([rows[:, :LANES] * free, rows[:, LANES:]], axis=1)


def fold(strip):
    total = strip[:, :LANES]
    for start in range(LANES, strip.shape[1], LANES):
        total = total + strip[:, start : start + LANES]
    return total


def is_upper(axis):
    return lax.axis_index(axis) % 2


def pick(upper, near, far):
    mask = jnp.full(near.shape, upper, jnp.int32) == 1
    return jnp.where(mask, near, far), jnp.where(mask, far, near)


def y_sides(upper, near_ref, far_ref, comp, plane):
    row = slice(plane, plane + 1)
    return pick(upper, near_ref[comp, row, :], far_ref[comp, row, :])


def x_side(upper, near_ref, far_ref, comp, elem, n_elem, end):
    rows = side_rows(comp, elem, n_elem)
    return pick(upper, near_ref[rows, :], far_ref[rows, :])[end]


def columns(y_col_ref, which):
    return [y_col_ref[which, j] for j in range(NODES)]


def column_sum(cols, row_of):
    total = None
    for j in range(NODES):
        part = cols[j] * jnp.broadcast_to(row_of(j), (NODES, LANES))
        total = part if total is None else total + part
    return total


def along_z(flat, table):
    high = flat.astype(jnp.bfloat16)
    low = (flat - high.astype(jnp.float32)).astype(jnp.bfloat16)
    both = jnp.dot(
        jnp.concatenate([high, low], axis=1), table, preferred_element_type=jnp.float32
    )
    return both[:, :LANES] + both[:, LANES:]


def main_kernel(*refs, elems, n_elem):
    v_refs, refs = refs[:2], refs[2:]
    if 0 in elems:
        ynear_ref, yfar_ref = refs[:2]
        refs = refs[2:]
    free_ref, elem_ref, half_ref, halfz_ref, zmat_ref, ycol_ref = refs[:6]
    u_ref, k_ref, square_ref = refs[6:9]
    grad_ref, stress_ref, side_ref, along_ref = refs[9:]
    comps, planes, size_y, size_z = u_ref.shape
    n_tile = size_z // LANES
    y_upper = is_upper("gy")
    square = jnp.zeros((NODES, LANES), jnp.float32)
    for place, elem in enumerate(elems):
        base = elem * NODES
        sub = slice(place * NODES, (place + 1) * NODES)
        for plane in range(planes):
            part = None
            for comp in range(comps):
                lo = hi = None
                if elem in (0, n_elem - 1):
                    lo, hi = y_sides(y_upper, ynear_ref, yfar_ref, comp, plane)
                strip = sum_z(row_sum_y(v_refs, lo, hi, comp, plane, elem, n_elem))
                strip = release(strip, free_ref[plane, base : base + NODES, :])
                u_ref[comp, plane, sub, :] = strip
                part = strip * strip if part is None else part + strip * strip
            if plane not in (0, ORDER):
                part = fold(part * halfz_ref[0:1, :])
                square = square + part * half_ref[plane, base : base + NODES, :]
    square_ref[...] = square

    rows = comps * planes * size_y
    for tile in range(n_tile):
        lanes = slice(tile * LANES, (tile + 1) * LANES)
        flat = u_ref[:, :, :, lanes].reshape(rows, LANES)
        grad_ref[:, :, :, lanes] = along_z(flat, zmat_ref[0]).reshape(
            comps, planes, size_y, LANES
        )

    def block(tile, place):
        lanes = pl.ds(pl.multiple_of(tile * LANES, LANES), LANES)
        base = place * NODES
        sub = slice(base, base + NODES)
        cols = columns(ycol_ref, 0)
        for c in range(3):
            for plane in range(NODES):
                along_ref[c, plane] = column_sum(
                    cols, lambda j: u_ref[c, plane, base + j : base + j + 1, lanes]
                )
        even, odd = [], []
        for comp in range(3):
            vals = [u_ref[comp, i, sub, lanes] for i in range(NODES)]
            even.append([vals[i] + vals[ORDER - i] for i in range(HALF)])
            odd.append([vals[i] - vals[ORDER - i] for i in range(HALF)])
        scale = elem_ref[elems[place] * NODES : (elems[place] + 1) * NODES, lanes]
        xsum = [[None] * HALF for _ in range(3)]
        xdif = [[None] * HALF for _ in range(3)]
        for pair in range(HALF):
            first = [combine(ODD[pair], odd[c]) for c in range(3)]
            second = [combine(EVEN[pair], even[c]) for c in range(3)]
            side_x = []
            for plane, sign in ((pair, 1), (ORDER - pair, -1)):
                gx = [first[c] + second[c] if sign > 0 else first[c] - second[c] for c in range(3)]
                gy = [along_ref[c, plane] for c in range(3)]
                gz = [grad_ref[c, plane, sub, lanes] for c in range(3)]
                shear = scale * float(LAME_SHEAR * WEIGHTS[plane])
                twice = scale * float(2.0 * LAME_SHEAR * WEIGHTS[plane])
                spread = (gx[0] + gy[1] + gz[2]) * (scale * float(LAME_FIRST * WEIGHTS[plane]))
                sxx = twice * gx[0] + spread
                syy = twice * gy[1] + spread
                szz = twice * gz[2] + spread
                sxy = shear * (gx[1] + gy[0])
                sxz = shear * (gx[2] + gz[0])
                syz = shear * (gy[2] + gz[1])
                side_x.append((sxx, sxy, sxz))
                for c, value in enumerate((sxz, syz, szz)):
                    stress_ref[c, plane, sub, lanes] = value
                for c, value in enumerate((sxy, syy, syz)):
                    side_ref[c, plane, :, :] = value
            for c in range(3):
                se = side_x[0][c] + side_x[1][c]
                so = side_x[0][c] - side_x[1][c]
                for i in range(HALF):
                    add_x = float(EVEN[pair][i]) * so
                    add_y = float(ODD[pair][i]) * se
                    xsum[c][i] = add_x if pair == 0 else xsum[c][i] + add_x
                    xdif[c][i] = add_y if pair == 0 else xdif[c][i] + add_y
        cols = columns(ycol_ref, 1)
        for c in range(3):
            for plane in range(NODES):
                i = min(plane, ORDER - plane)
                total = xsum[c][i] + xdif[c][i] if plane < HALF else xsum[c][i] - xdif[c][i]
                k_ref[c, plane, sub, lanes] = total + column_sum(
                    cols, lambda b: side_ref[c, plane, b : b + 1, :]
                )

    @pl.loop(0, n_tile)
    def _(tile):
        for place in range(len(elems)):
            block(tile, place)

    for tile in range(n_tile):
        lanes = slice(tile * LANES, (tile + 1) * LANES)
        flat = stress_ref[:, :, :, lanes].reshape(rows, LANES)
        k_ref[:, :, :, lanes] += along_z(flat, zmat_ref[1]).reshape(comps, planes, size_y, LANES)


SHEAR, FIRST = float(LAME_SHEAR), float(LAME_FIRST)
DIAG = 2.0 * SHEAR + FIRST
ENDS = (0, ORDER)
THROUGH = np.einsum("ai,a,ap->ip", DERIV, WEIGHTS, DERIV)
ONWARD = DERIV.T
BACKWARD = WEIGHTS[:, None] * DERIV


def spread_pair(total_p, total_m, table, i, sign, even, odd):
    alpha = 0.5 * float(table[i, 0] + table[i, ORDER]) * even
    beta = 0.5 * float(table[i, 0] - table[i, ORDER]) * odd
    plus, minus = (alpha, beta) if sign > 0 else (beta, alpha)
    if total_p is None:
        return plus, minus
    return total_p + plus, total_m + minus


def update_kernel(*refs, elems, n_elem, slot, last):
    u_ref, kin_ref, xnear_ref, xfar_ref = refs[:4]
    free_ref, elem_ref, half_ref, halfz_ref, zmat_ref, ycol_ref = refs[4:10]
    outer = 0 in elems
    squares_refs, refs = refs[10:12], refs[12:]
    if not outer:
        uo_ref, ko_ref, fo_ref, carry_ref = refs[:4]
        refs = refs[4:]
    k_ref, face_ref = refs[:2]
    refs = refs[2:]
    if not outer:
        sums_ref, *refs = refs
    if outer:
        near_ref, far_ref = refs[:2]
        refs = refs[2:]
    add_ref, grad_ref, keep_ref, zin_ref, zout_ref, side_ref = refs
    comps, planes, size_y, size_z = k_ref.shape
    n_tile = size_z // LANES
    x_upper = is_upper("gx")
    for place, elem in enumerate(elems):
        rows = slice(elem * NODES, (elem + 1) * NODES)
        own = slice(place * NODES, (place + 1) * NODES)
        for end, plane in enumerate(ENDS):
            for comp in range(comps):
                strip = x_side(x_upper, xnear_ref, xfar_ref, comp, elem, n_elem, end)
                strip = release(sum_z(strip), free_ref[plane, rows, :])
                add_ref[comp, end, own, :] = strip
                face_ref[comp, end, own, :] = strip + u_ref[comp, plane, own, :]

    for tile in range(n_tile):
        lanes = slice(tile * LANES, (tile + 1) * LANES)
        flat = add_ref[:, :, :, lanes].reshape(comps * 2 * size_y, LANES)
        grad_ref[:, :, :, lanes] = along_z(flat, zmat_ref[0]).reshape(comps, 2, size_y, LANES)

    @pl.loop(0, n_tile)
    def _(tile):
        lanes = pl.ds(pl.multiple_of(tile * LANES, LANES), LANES)
        for place, elem in enumerate(elems):
            base = place * NODES
            sub = slice(base, base + NODES)
            scale = elem_ref[elem * NODES : (elem + 1) * NODES, lanes]
            cols = columns(ycol_ref, 0)
            for end, plane in enumerate(ENDS):
                gy = [
                    column_sum(
                        cols, lambda j: add_ref[c, end, base + j : base + j + 1, lanes]
                    )
                    for c in range(3)
                ]
                gz = [grad_ref[c, end, sub, lanes] for c in range(3)]
                own = scale * float(WEIGHTS[plane])
                axx = own * (FIRST * (gy[1] + gz[2]))
                axy = own * (SHEAR * gy[0])
                axz = own * (SHEAR * gz[0])
                ayy = own * (DIAG * gy[1] + FIRST * gz[2])
                azz = own * (DIAG * gz[2] + FIRST * gy[1])
                ayz = own * (SHEAR * (gy[2] + gz[1]))
                scaled = [scale * add_ref[c, end, sub, lanes] for c in range(3)]
                for c, value in enumerate((SHEAR * scaled[2], FIRST * scaled[0], axz, ayz, azz)):
                    zin_ref[c, end, sub, lanes] = value
                for c, value in enumerate((SHEAR * scaled[1], FIRST * scaled[0], axy, ayy, ayz)):
                    side_ref[c, end, :, :] = value
                for c, value in enumerate((axx, axy, axz)):
                    keep_ref[c, end, sub, lanes] = value
            cols = columns(ycol_ref, 1)
            for end in range(2):
                for c in range(5):
                    keep_ref[3 + c, end, sub, lanes] = column_sum(
                        cols, lambda b: side_ref[c, end, b : b + 1, :]
                    )

    for tile in range(n_tile):
        lanes = slice(tile * LANES, (tile + 1) * LANES)
        flat = zin_ref[:, :, :, lanes].reshape(5 * 2 * size_y, LANES)
        zout_ref[:, :, :, lanes] = along_z(flat, zmat_ref[1]).reshape(5, 2, size_y, LANES)

    def tile_energy(tile, energy):
        lanes = pl.ds(pl.multiple_of(tile * LANES, LANES), LANES)
        if not outer:
            for plane in range(planes):
                for c in range(comps):
                    vector = uo_ref[c, plane, :, lanes]
                    if plane in ENDS:
                        vector = fo_ref[c, ENDS.index(plane), :, lanes]
                    product = vector * ko_ref[c, plane, :, lanes]
                    energy = energy + product[:NODES] + product[NODES:]
        for place, elem in enumerate(elems):
            sub = slice(place * NODES, (place + 1) * NODES)
            scale = elem_ref[elem * NODES : (elem + 1) * NODES, lanes]
            zout = [[zout_ref[c, end, sub, lanes] for end in range(2)] for c in range(5)]
            kept = [[keep_ref[c, end, sub, lanes] for end in range(2)] for c in range(8)]
            back = (
                [kept[3][end] + zout[0][end] for end in range(2)],
                kept[4],
                zout[1],
            )
            for c in range(3):
                factor = scale * (DIAG if c == 0 else SHEAR)
                pairs = (
                    ([factor * add_ref[c, end, sub, lanes] for end in range(2)], THROUGH, 1),
                    (kept[c], ONWARD, -1),
                    (back[c], BACKWARD, -1),
                )
                pairs = [(v[0] + v[1], v[0] - v[1], table, sign) for v, table, sign in pairs]
                for i in range(HALF):
                    plus = minus = None
                    for even, odd, table, sign in pairs:
                        plus, minus = spread_pair(plus, minus, table, i, sign, even, odd)
                    for plane, value in ((i, plus + minus), (ORDER - i, plus - minus)):
                        value = value + kin_ref[c, plane, sub, lanes]
                        if plane in ENDS:
                            end = ENDS.index(plane)
                            value = value + (kept[5 + c][end] + zout[2 + c][end])
                            vector = None if outer else face_ref[c, end, sub, lanes]
                        elif not outer:
                            vector = u_ref[c, plane, sub, lanes]
                        k_ref[c, plane, sub, lanes] = value
                        if not outer:
                            energy = energy + value * vector
        return energy

    energy = lax.fori_loop(0, n_tile, tile_energy, jnp.zeros((NODES, LANES), jnp.float32))
    if outer:
        put_rows(
            lambda comp, plane: k_ref[comp, plane, 0:1, :],
            lambda comp, plane: k_ref[comp, plane, size_y - 1 : size_y, :],
            near_ref,
            far_ref,
        )
        return
    square = squares_refs[0][...] + squares_refs[1][...]
    for group, ref in ((elems, face_ref), ((0, n_elem - 1), fo_ref)):
        for place, elem in enumerate(group):
            own = slice(place * NODES, (place + 1) * NODES)
            rows = slice(elem * NODES, (elem + 1) * NODES)
            for end, plane in enumerate(ENDS):
                part = None
                for comp in range(comps):
                    strip = ref[comp, end, own, :]
                    part = strip * strip if part is None else part + strip * strip
                square = square + fold(part * halfz_ref[0:1, :]) * half_ref[plane, rows, :]
    moments = [carry_ref[i] for i in range(4)]
    moments[2 * slot] = moments[2 * slot] + square
    moments[2 * slot + 1] = moments[2 * slot + 1] + energy
    if not last:
        for i in range(4):
            sums_ref[i] = moments[i]
    else:
        lane = lax.broadcasted_iota(jnp.int32, sums_ref.shape, 1)
        known = jnp.zeros(sums_ref.shape, jnp.float32)
        for i in range(4):
            known = jnp.where(lane == i, jnp.sum(moments[i]), known)
        sums_ref[...] = known


def put_rows(lo_of, hi_of, near_ref, far_ref):
    y_upper = is_upper("gy")
    comps, planes, _ = near_ref.shape
    for comp in range(comps):
        for plane in range(planes):
            row = slice(plane, plane + 1)
            far_ref[comp, row, :], near_ref[comp, row, :] = pick(
                y_upper, hi_of(comp, plane), lo_of(comp, plane)
            )


def scale_kernel(flags_ref, widen_ref, weight_ref, scale_ref):
    solid = (flags_ref[...] == 1).astype(jnp.bfloat16)
    solid = jnp.dot(solid, widen_ref[...], preferred_element_type=jnp.float32)
    modulus = jnp.where(solid > 0.5, SOLID_MODULUS, VOID_MODULUS).astype(jnp.float32)
    for elem in range(flags_ref.shape[0]):
        scale_ref[elem * NODES : (elem + 1) * NODES, :] = (
            modulus[elem : elem + 1, :] * weight_ref[...]
        )


def rows_kernel(v_ref, near_ref, far_ref):
    size_y = v_ref.shape[2]
    put_rows(
        lambda comp, plane: v_ref[comp, plane, 0:1, :],
        lambda comp, plane: v_ref[comp, plane, size_y - 1 : size_y, :],
        near_ref,
        far_ref,
    )


def side_rows(comp, elem, n_elem):
    start = comp * (n_elem * ORDER + 1) + elem * ORDER
    return slice(start, start + NODES)


def faces_kernel(*refs, n_elem):
    vmid_ref, vedge_ref, ynear_ref, yfar_ref = refs[:4]
    near_ref, far_ref = refs[-2:]
    comps = vmid_ref.shape[0]
    x_upper, y_upper = is_upper("gx"), is_upper("gy")
    v_refs = vmid_ref, vedge_ref
    for comp in range(comps):
        sides = [y_sides(y_upper, ynear_ref, yfar_ref, comp, plane) for plane in ENDS]
        for elem in range(n_elem):
            rows = side_rows(comp, elem, n_elem)
            lo, hi = [
                row_sum_y(v_refs, *side, comp, plane, elem, n_elem)
                for plane, side in zip(ENDS, sides)
            ]
            near_ref[rows, :], far_ref[rows, :] = pick(x_upper, lo, hi)


def assemble_kernel(kmid_ref, kedge_ref, free_ref, w_ref, done_ref, *, elems, n_elem):
    for place, elem in enumerate(elems):
        own = slice(place * NODES, (place + 1) * NODES)
        sub = slice(elem * NODES, (elem + 1) * NODES)
        for plane in range(w_ref.shape[1]):
            for comp in range(w_ref.shape[0]):
                rows = row_sum_y((kmid_ref, kedge_ref), None, None, comp, plane, elem, n_elem)
                w_ref[comp, plane, own, :] = release(sum_z(rows), free_ref[plane, sub, :])
    done_ref[...] = w_ref[0, 0, 0:NODES, :LANES]


def finish_kernel(*refs):
    *k_refs, w_ref = refs[:3]
    ynear_ref, yfar_ref, xnear_ref, xfar_ref, free_ref = refs[3:8]
    r_refs, r_faces, q_refs, q_faces = refs[8:10], refs[10:12], refs[12:14], refs[14:16]
    sums_ref, adj_out, res_out, adj_ref, res_ref, sem_ref = refs[16:]
    planes, comps, size_y, _ = adj_ref.shape
    n_elem = size_y // NODES
    x_upper, y_upper = is_upper("gx"), is_upper("gy")
    sums = jnp.sum(sums_ref[...], axis=0, keepdims=True)
    lane = lax.broadcasted_iota(jnp.int32, sums.shape, 1)
    m0, m1, m2, m3 = [
        jnp.sum(jnp.where(lane == i, sums, 0.0), axis=1, keepdims=True) for i in range(4)
    ]
    first = m0 / m1
    following = first * first * m2 - m0
    ratio = following / m0
    grow = 1.0 + ratio
    second = following / (grow * grow * m1 - 2.0 * first * grow * m2 + first * first * m3)
    lead = first + second * grow
    cross = first * second
    copies = []
    for plane in range(planes):
        end = ENDS.index(plane) if plane in ENDS else None
        place = plane if end is None else end
        for comp in range(comps):
            for elem in range(n_elem):
                sub = slice(elem * NODES, (elem + 1) * NODES)
                r_ref, row = locate(r_refs if end is None else r_faces, elem, n_elem)
                q_ref, row = locate(q_refs if end is None else q_faces, elem, n_elem)
                own = slice(row, row + NODES)
                strip = None
                if end is not None:
                    strip = x_side(x_upper, xnear_ref, xfar_ref, comp, elem, n_elem, end)
                if elem in (0, n_elem - 1):
                    lo, hi = y_sides(y_upper, ynear_ref, yfar_ref, comp, plane)
                    rows = row_sum_y(k_refs, lo, hi, comp, plane, elem, n_elem)
                    strip = rows if strip is None else strip + rows
                if strip is not None:
                    strip = release(sum_z(strip), free_ref[plane, sub, :])
                if elem not in (0, n_elem - 1):
                    rows = w_ref[comp, plane, own, :]
                    strip = rows if strip is None else strip + rows
                loads = r_ref[comp, place, own, :]
                image = q_ref[comp, place, own, :]
                adj_ref[plane, comp, sub, :] = lead * loads - cross * image
                res_ref[plane, comp, sub, :] = loads - lead * image + cross * strip
        for which, (ref, out) in enumerate(((adj_ref, adj_out), (res_ref, res_out))):
            copy = pltpu.make_async_copy(ref.at[plane], out.at[:, plane], sem_ref.at[which, plane])
            copy.start()
            copies.append(copy)
    for copy in copies:
        copy.wait()


def swap(near_out, far_out, axis):
    count = lax.axis_size(axis)
    inner = [(i, i ^ 1) for i in range(count)]
    outer = [(i, ((i + 1) ^ 1) - 1) for i in range(1, count - 1)]
    far = lax.ppermute(far_out, axis, outer)
    near = lax.ppermute(near_out, axis, inner)
    return near, far


def local(rhs_loads, flags, fixed):
    comps, size_x, size_y, size_z = rhs_loads.shape
    axes = ("gx", "gy")
    devices = lax.axis_size("gx") * lax.axis_size("gy")
    f32 = jnp.float32
    y_side = jax.ShapeDtypeStruct((comps, size_x, size_z), f32)
    side_len = comps * (size_y // NODES * ORDER + 1)
    side = jax.ShapeDtypeStruct((side_len + -side_len % NODES, size_z), f32)
    whole = pl.BlockSpec(memory_space=pltpu.VMEM)

    n_elem, n_deep = flags.shape[1:]
    widen = jnp.asarray(np.kron(np.eye(n_deep), np.ones((1, NODES))), jnp.bfloat16)
    weight_yz = jnp.asarray(WEIGHTS[:, None] * np.tile(WEIGHTS, n_deep)[None, :], f32)
    elem_scale = pl.pallas_call(
        scale_kernel,
        in_specs=[whole] * 3,
        out_specs=whole,
        out_shape=jax.ShapeDtypeStruct((size_y, size_z), f32),
        compiler_params=pltpu.CompilerParams(vmem_limit_bytes=VMEM_LIMIT),
        cost_estimate=pl.CostEstimate(flops=1000, bytes_accessed=100000, transcendentals=0),
        name="scale",
    )(flags[0], widen, weight_yz)
    free = 1.0 - fixed.astype(f32)[:, :, None] * (jnp.arange(LANES) == 0).astype(f32)
    half_xy = (
        shared_halves(size_x, lax.axis_index("gx") * size_x, size_x * lax.axis_size("gx"), NODES)[
            :, None, None
        ]
        * shared_halves(
            size_y, lax.axis_index("gy") * size_y, size_y * lax.axis_size("gy"), NODES
        )[None, :, None]
        * jnp.ones((LANES,), f32)
    )
    half_z = jnp.broadcast_to(shared_halves(size_z, 0, size_z, NODES)[None], (NODES, size_z))
    z_mat = jnp.asarray(np.stack([z_table(DERIV.T), z_table(DERIV)]))
    y_col = jnp.asarray(
        np.broadcast_to(
            np.stack([DERIV.T, DERIV])[:, :, :, None], (2, NODES, NODES, LANES)
        ),
        f32,
    )

    mid, edge = parts(n_elem)
    tables = (free, elem_scale, half_xy, half_z, z_mat, y_col)

    def shape(*sizes):
        return jax.ShapeDtypeStruct(sizes, f32)

    def call(
        kernel, name, args, out_shape, scratch=(), us=1.0, out_spec=whole
    ):
        return pl.pallas_call(
            kernel,
            in_specs=[whole] * len(args),
            out_specs=[out_spec] * len(out_shape),
            out_shape=list(out_shape),
            scratch_shapes=list(scratch),
            compiler_params=pltpu.CompilerParams(vmem_limit_bytes=VMEM_LIMIT),
            cost_estimate=pl.CostEstimate(
                flops=int(us * 4e6), bytes_accessed=int(us * 2.5e6), transcendentals=0
            ),
            name=name,
        )(*args)

    def main(v, y_halo, elems, name):
        some = (comps, size_x, len(elems) * NODES, size_z)
        return call(
            functools.partial(main_kernel, elems=elems, n_elem=n_elem),
            name,
            (*v, *y_halo, *tables),
            (shape(*some), shape(*some), shape(NODES, LANES)),
            (
                pltpu.VMEM(some, f32),
                pltpu.VMEM(some, f32),
                pltpu.VMEM((comps, size_x, NODES, LANES), f32),
                pltpu.VMEM((comps, size_x, NODES, LANES), f32),
            ),
            us=5.0,
        )

    def update(u, k, x_halo, squares, others, elems, slot, name):
        rows = len(elems) * NODES
        last = slot == 1 and 0 not in elems
        out = [shape(comps, size_x, rows, size_z), shape(comps, 2, rows, size_z)]
        if 0 in elems:
            out += [y_side, y_side]
        else:
            out += [shape(devices, LANES) if last else shape(4, NODES, LANES)]
        return call(
            functools.partial(update_kernel, elems=elems, n_elem=n_elem, slot=slot, last=last),
            name,
            (u, k, *x_halo, *tables, *squares, *others),
            out,
            (
                pltpu.VMEM((comps, 2, rows, size_z), f32),
                pltpu.VMEM((comps, 2, rows, size_z), f32),
                pltpu.VMEM((8, 2, rows, size_z), f32),
                pltpu.VMEM((5, 2, rows, size_z), f32),
                pltpu.VMEM((5, 2, rows, size_z), f32),
                pltpu.VMEM((5, 2, NODES, LANES), f32),
            ),
            us=2.0,
        )

    def y_halos(y_rows):
        return swap(*y_rows, "gy")

    def x_halos(v, y_halo, after):
        sides = call(
            functools.partial(faces_kernel, n_elem=n_elem),
            "faces",
            (*v, *y_halo, *after),
            (side, side),
            us=0.3,
        )
        return swap(*sides, "gx")

    def step(v, y_rows, carry, slot):
        y_halo = y_halos(y_rows)
        u_mid, k_mid, sq_mid = main(v, (), mid, "middle")
        x_halo = x_halos(v, y_halo, ())
        u_edge, k_edge, sq_edge = main(v, y_halo, edge, "edges")
        squares = sq_mid, sq_edge
        k_edge, f_edge, *y_rows = update(
            u_edge, k_edge, x_halo, squares, (), edge, slot, "update_edges"
        )
        outer = u_edge, k_edge, f_edge, carry
        k_mid, f_mid, carry = update(
            u_mid, k_mid, x_halo, squares, outer, mid, slot, "update_middle"
        )
        return (k_mid, k_edge), (u_mid, u_edge, f_mid, f_edge), y_rows, carry

    y_rows = call(rows_kernel, "rows", (rhs_loads,), (y_side, y_side), us=0.1)
    carry = jnp.zeros((4, NODES, LANES), f32)
    k_loads, loads, y_rows, carry = step((rhs_loads, rhs_loads), y_rows, carry, 0)
    k_image, image, y_rows, sums = step(k_loads, y_rows, carry, 1)
    y_halo = y_halos(y_rows)
    w_mid, done = call(
        functools.partial(assemble_kernel, elems=mid, n_elem=n_elem),
        "assemble",
        (*k_image, free),
        (shape(comps, size_x, len(mid) * NODES, size_z), shape(NODES, LANES)),
        us=1.0,
    )
    x_halo = x_halos(k_image, y_halo, (done,))
    sums = lax.all_to_all(sums, axes, 0, 0, tiled=True)
    return tuple(
        call(
            finish_kernel,
            "finish",
            (*k_image, w_mid, *y_halo, *x_halo, free, *loads, *image, sums),
            (shape(*rhs_loads.shape),) * 2,
            (
                pltpu.VMEM((size_x, comps, size_y, size_z), f32),
                pltpu.VMEM((size_x, comps, size_y, size_z), f32),
                pltpu.SemaphoreType.DMA((2, size_x)),
            ),
            us=4.0,
            out_spec=pl.BlockSpec(memory_space=pltpu.HBM),
        )
    )


def solution(mesh):
    in_specs = (P(None, "gx", "gy", None), P("gx", "gy", None), P("gx", "gy"))
    out_specs = (P(None, "gx", "gy", None), P(None, "gx", "gy", None))
    return jax.shard_map(local, mesh=mesh, in_specs=in_specs, out_specs=out_specs, check_vma=False)
```

```python
import functools

import jax
import jax.numpy as jnp
import numpy as np
from jax import lax
from jax.experimental import pallas as pl
from jax.experimental.pallas import tpu as pltpu
from jax.sharding import PartitionSpec as P

ORDER = 7
NODES = ORDER + 1
LANES = 128

POISSON = 0.3
LAME_FIRST = POISSON / ((1.0 + POISSON) * (1.0 - 2.0 * POISSON))
LAME_SHEAR = 1.0 / (2.0 * (1.0 + POISSON))
SOLID_MODULUS = 0.1
VOID_MODULUS = 0.001
INTERIOR_POINTS = (
    -0.8717401485096066,
    -0.5917001814331423,
    -0.2092992179024789,
    0.2092992179024789,
    0.5917001814331423,
    0.8717401485096066,
)
VMEM_LIMIT = 10 * 1024 * 1024


def legendre_value(poly_order, point):
    previous = 1.0
    current = point
    for degree in range(1, poly_order):
        following = ((2.0 * degree + 1.0) * point * current - degree * previous) / (degree + 1.0)
        previous = current
        current = following
    return current


def gll_tables(poly_order):
    points = np.array([-1.0] + list(INTERIOR_POINTS) + [1.0])
    values = np.array([legendre_value(poly_order, float(point)) for point in points])
    weights = 2.0 / (poly_order * (poly_order + 1) * values**2)
    node_count = poly_order + 1
    derivative = np.zeros((node_count, node_count))
    for row_index in range(node_count):
        for col_index in range(node_count):
            if row_index != col_index:
                derivative[row_index, col_index] = values[row_index] / (
                    values[col_index] * (points[row_index] - points[col_index])
                )
    derivative[0, 0] = -poly_order * (poly_order + 1) / 4.0
    derivative[poly_order, poly_order] = poly_order * (poly_order + 1) / 4.0
    return (derivative, weights)


DERIV, WEIGHTS = gll_tables(ORDER)
HALF = NODES // 2
ODD = [[0.5 * (DERIV[a, i] - DERIV[a, ORDER - i]) for i in range(HALF)] for a in range(HALF)]
EVEN = [[0.5 * (DERIV[a, i] + DERIV[a, ORDER - i]) for i in range(HALF)] for a in range(HALF)]


def z_table(matrix):
    blocks = np.kron(np.eye(LANES // NODES), matrix).astype(np.float32)
    high = blocks.astype(jnp.bfloat16)
    low = (blocks - high.astype(np.float32)).astype(jnp.bfloat16)
    row = np.concatenate([high, low], axis=1)
    return np.concatenate([row, row], axis=0)


def shared_halves(local_len, offset, global_len, node_count):
    position = jnp.arange(local_len, dtype=jnp.int32)
    node_index = position % node_count
    global_pos = position + offset
    shared = (node_index == 0) & (global_pos > 0) | (node_index == node_count - 1) & (
        global_pos < global_len - 1
    )
    return jnp.where(shared, 0.5, 1.0).astype(jnp.float32)


def combine(coefs, terms):
    total = None
    for coef, term in zip(coefs, terms):
        part = float(coef) * term
        total = part if total is None else total + part
    return total


def parts(n_elem):
    return tuple(range(1, n_elem - 1)), (0, n_elem - 1)


def locate(refs, elem, n_elem):
    if refs[0].shape[2] == n_elem * NODES:
        return refs[0], elem * NODES
    for ref, group in zip(refs, parts(n_elem)):
        if elem in group:
            return ref, group.index(elem) * NODES


def row_sum_y(refs, lo, hi, comp, plane, elem, n_elem):
    ref, base = locate(refs, elem, n_elem)
    own = ref[comp, plane, base : base + NODES, :]
    if elem > 0:
        ref, base = locate(refs, elem - 1, n_elem)
        lo = ref[comp, plane, base + ORDER : base + NODES, :]
    if elem < n_elem - 1:
        ref, base = locate(refs, elem + 1, n_elem)
        hi = ref[comp, plane, base : base + 1, :]
    sub = lax.broadcasted_iota(jnp.int32, own.shape, 0)
    lo = jnp.broadcast_to(lo, own.shape)
    hi = jnp.broadcast_to(hi, own.shape)
    return own + jnp.where(sub == 0, lo, jnp.where(sub == ORDER, hi, 0.0))


def sum_z(rows):
    size = rows.shape[-1]
    lane = lax.broadcasted_iota(jnp.int32, rows.shape, 1)
    ahead = pltpu.roll(rows, size - 1, 1)
    behind = pltpu.roll(rows, 1, 1)
    upper = (lane % NODES == ORDER) & (lane < size - 1)
    lower = (lane % NODES == 0) & (lane > 0)
    return rows + jnp.where(upper, ahead, jnp.where(lower, behind, 0.0))


def release(rows, free):
    return jnp.concatenate([rows[:, :LANES] * free, rows[:, LANES:]], axis=1)


def fold(strip):
    total = strip[:, :LANES]
    for start in range(LANES, strip.shape[1], LANES):
        total = total + strip[:, start : start + LANES]
    return total


def is_upper(axis):
    return lax.axis_index(axis) % 2


def pick(upper, near, far):
    mask = jnp.full(near.shape, upper, jnp.int32) == 1
    return jnp.where(mask, near, far), jnp.where(mask, far, near)


def y_sides(upper, near_ref, far_ref, comp, plane):
    row = slice(plane, plane + 1)
    return pick(upper, near_ref[comp, row, :], far_ref[comp, row, :])


def x_side(upper, near_ref, far_ref, comp, elem, n_elem, end):
    rows = side_rows(comp, elem, n_elem)
    return pick(upper, near_ref[rows, :], far_ref[rows, :])[end]


def columns(y_col_ref, which):
    return [y_col_ref[which, j] for j in range(NODES)]


def column_sum(cols, row_of):
    total = None
    for j in range(NODES):
        part = cols[j] * jnp.broadcast_to(row_of(j), (NODES, LANES))
        total = part if total is None else total + part
    return total


def along_z(flat, table):
    high = flat.astype(jnp.bfloat16)
    low = (flat - high.astype(jnp.float32)).astype(jnp.bfloat16)
    both = jnp.dot(
        jnp.concatenate([high, low], axis=1), table, preferred_element_type=jnp.float32
    )
    return both[:, :LANES] + both[:, LANES:]


def main_kernel(*refs, elems, n_elem):
    v_refs, refs = refs[:2], refs[2:]
    if 0 in elems:
        ynear_ref, yfar_ref = refs[:2]
        refs = refs[2:]
    free_ref, elem_ref, half_ref, halfz_ref, zmat_ref, ycol_ref = refs[:6]
    u_ref, k_ref, square_ref = refs[6:9]
    grad_ref, stress_ref, side_ref, along_ref = refs[9:]
    comps, planes, size_y, size_z = u_ref.shape
    n_tile = size_z // LANES
    y_upper = is_upper("gy")
    square = jnp.zeros((NODES, LANES), jnp.float32)
    for place, elem in enumerate(elems):
        base = elem * NODES
        sub = slice(place * NODES, (place + 1) * NODES)
        for plane in range(planes):
            part = None
            for comp in range(comps):
                lo = hi = None
                if elem in (0, n_elem - 1):
                    lo, hi = y_sides(y_upper, ynear_ref, yfar_ref, comp, plane)
                strip = sum_z(row_sum_y(v_refs, lo, hi, comp, plane, elem, n_elem))
                strip = release(strip, free_ref[plane, base : base + NODES, :])
                u_ref[comp, plane, sub, :] = strip
                part = strip * strip if part is None else part + strip * strip
            if plane not in (0, ORDER):
                part = fold(part * halfz_ref[0:1, :])
                square = square + part * half_ref[plane, base : base + NODES, :]
    square_ref[...] = square

    rows = comps * planes * size_y
    for tile in range(n_tile):
        lanes = slice(tile * LANES, (tile + 1) * LANES)
        flat = u_ref[:, :, :, lanes].reshape(rows, LANES)
        grad_ref[:, :, :, lanes] = along_z(flat, zmat_ref[0]).reshape(
            comps, planes, size_y, LANES
        )

    def block(tile, place):
        lanes = pl.ds(pl.multiple_of(tile * LANES, LANES), LANES)
        base = place * NODES
        sub = slice(base, base + NODES)
        cols = columns(ycol_ref, 0)
        for c in range(3):
            for plane in range(NODES):
                along_ref[c, plane] = column_sum(
                    cols, lambda j: u_ref[c, plane, base + j : base + j + 1, lanes]
                )
        even, odd = [], []
        for comp in range(3):
            vals = [u_ref[comp, i, sub, lanes] for i in range(NODES)]
            even.append([vals[i] + vals[ORDER - i] for i in range(HALF)])
            odd.append([vals[i] - vals[ORDER - i] for i in range(HALF)])
        scale = elem_ref[elems[place] * NODES : (elems[place] + 1) * NODES, lanes]
        xsum = [[None] * HALF for _ in range(3)]
        xdif = [[None] * HALF for _ in range(3)]
        for pair in range(HALF):
            first = [combine(ODD[pair], odd[c]) for c in range(3)]
            second = [combine(EVEN[pair], even[c]) for c in range(3)]
            side_x = []
            for plane, sign in ((pair, 1), (ORDER - pair, -1)):
                gx = [first[c] + second[c] if sign > 0 else first[c] - second[c] for c in range(3)]
                gy = [along_ref[c, plane] for c in range(3)]
                gz = [grad_ref[c, plane, sub, lanes] for c in range(3)]
                shear = scale * float(LAME_SHEAR * WEIGHTS[plane])
                twice = scale * float(2.0 * LAME_SHEAR * WEIGHTS[plane])
                spread = (gx[0] + gy[1] + gz[2]) * (scale * float(LAME_FIRST * WEIGHTS[plane]))
                sxx = twice * gx[0] + spread
                syy = twice * gy[1] + spread
                szz = twice * gz[2] + spread
                sxy = shear * (gx[1] + gy[0])
                sxz = shear * (gx[2] + gz[0])
                syz = shear * (gy[2] + gz[1])
                side_x.append((sxx, sxy, sxz))
                for c, value in enumerate((sxz, syz, szz)):
                    stress_ref[c, plane, sub, lanes] = value
                for c, value in enumerate((sxy, syy, syz)):
                    side_ref[c, plane, :, :] = value
            for c in range(3):
                se = side_x[0][c] + side_x[1][c]
                so = side_x[0][c] - side_x[1][c]
                for i in range(HALF):
                    add_x = float(EVEN[pair][i]) * so
                    add_y = float(ODD[pair][i]) * se
                    xsum[c][i] = add_x if pair == 0 else xsum[c][i] + add_x
                    xdif[c][i] = add_y if pair == 0 else xdif[c][i] + add_y
        cols = columns(ycol_ref, 1)
        for c in range(3):
            for plane in range(NODES):
                i = min(plane, ORDER - plane)
                total = xsum[c][i] + xdif[c][i] if plane < HALF else xsum[c][i] - xdif[c][i]
                k_ref[c, plane, sub, lanes] = total + column_sum(
                    cols, lambda b: side_ref[c, plane, b : b + 1, :]
                )

    @pl.loop(0, n_tile)
    def _(tile):
        for place in range(len(elems)):
            block(tile, place)

    for tile in range(n_tile):
        lanes = slice(tile * LANES, (tile + 1) * LANES)
        flat = stress_ref[:, :, :, lanes].reshape(rows, LANES)
        k_ref[:, :, :, lanes] += along_z(flat, zmat_ref[1]).reshape(comps, planes, size_y, LANES)


SHEAR, FIRST = float(LAME_SHEAR), float(LAME_FIRST)
DIAG = 2.0 * SHEAR + FIRST
ENDS = (0, ORDER)
THROUGH = np.einsum("ai,a,ap->ip", DERIV, WEIGHTS, DERIV)
ONWARD = DERIV.T
BACKWARD = WEIGHTS[:, None] * DERIV


def spread_pair(total_p, total_m, table, i, sign, even, odd):
    alpha = 0.5 * float(table[i, 0] + table[i, ORDER]) * even
    beta = 0.5 * float(table[i, 0] - table[i, ORDER]) * odd
    plus, minus = (alpha, beta) if sign > 0 else (beta, alpha)
    if total_p is None:
        return plus, minus
    return total_p + plus, total_m + minus


def update_kernel(*refs, elems, n_elem, slot, last):
    u_ref, kin_ref, xnear_ref, xfar_ref = refs[:4]
    free_ref, elem_ref, half_ref, halfz_ref, zmat_ref, ycol_ref = refs[4:10]
    outer = 0 in elems
    squares_refs, refs = refs[10:12], refs[12:]
    if not outer:
        uo_ref, ko_ref, fo_ref, carry_ref = refs[:4]
        refs = refs[4:]
    k_ref, face_ref = refs[:2]
    refs = refs[2:]
    if not outer:
        sums_ref, *refs = refs
    if outer:
        near_ref, far_ref = refs[:2]
        refs = refs[2:]
    add_ref, grad_ref, keep_ref, zin_ref, zout_ref, side_ref = refs
    comps, planes, size_y, size_z = k_ref.shape
    n_tile = size_z // LANES
    x_upper = is_upper("gx")
    for place, elem in enumerate(elems):
        rows = slice(elem * NODES, (elem + 1) * NODES)
        own = slice(place * NODES, (place + 1) * NODES)
        for end, plane in enumerate(ENDS):
            for comp in range(comps):
                strip = x_side(x_upper, xnear_ref, xfar_ref, comp, elem, n_elem, end)
                strip = release(sum_z(strip), free_ref[plane, rows, :])
                add_ref[comp, end, own, :] = strip
                face_ref[comp, end, own, :] = strip + u_ref[comp, plane, own, :]

    for tile in range(n_tile):
        lanes = slice(tile * LANES, (tile + 1) * LANES)
        flat = add_ref[:, :, :, lanes].reshape(comps * 2 * size_y, LANES)
        grad_ref[:, :, :, lanes] = along_z(flat, zmat_ref[0]).reshape(comps, 2, size_y, LANES)
        for place, elem in enumerate(elems):
            base = place * NODES
            sub = slice(base, base + NODES)
            scale = elem_ref[elem * NODES : (elem + 1) * NODES, lanes]
            cols = columns(ycol_ref, 0)
            for end, plane in enumerate(ENDS):
                gy = [
                    column_sum(
                        cols, lambda j: add_ref[c, end, base + j : base + j + 1, lanes]
                    )
                    for c in range(3)
                ]
                gz = [grad_ref[c, end, sub, lanes] for c in range(3)]
                own = scale * float(WEIGHTS[plane])
                axx = own * (FIRST * (gy[1] + gz[2]))
                axy = own * (SHEAR * gy[0])
                axz = own * (SHEAR * gz[0])
                ayy = own * (DIAG * gy[1] + FIRST * gz[2])
                azz = own * (DIAG * gz[2] + FIRST * gy[1])
                ayz = own * (SHEAR * (gy[2] + gz[1]))
                scaled = [scale * add_ref[c, end, sub, lanes] for c in range(3)]
                for c, value in enumerate((SHEAR * scaled[2], FIRST * scaled[0], axz, ayz, azz)):
                    zin_ref[c, end, sub, lanes] = value
                for c, value in enumerate((SHEAR * scaled[1], FIRST * scaled[0], axy, ayy, ayz)):
                    side_ref[c, end, :, :] = value
                for c, value in enumerate((axx, axy, axz)):
                    keep_ref[c, end, sub, lanes] = value
            cols = columns(ycol_ref, 1)
            for end in range(2):
                for c in range(5):
                    keep_ref[3 + c, end, sub, lanes] = column_sum(
                        cols, lambda b: side_ref[c, end, b : b + 1, :]
                    )
        flat = zin_ref[:, :, :, lanes].reshape(5 * 2 * size_y, LANES)
        zout_ref[:, :, :, lanes] = along_z(flat, zmat_ref[1]).reshape(5, 2, size_y, LANES)

    def tile_energy(tile, energy):
        lanes = slice(tile * LANES, (tile + 1) * LANES)
        if not outer:
            for plane in range(planes):
                for c in range(comps):
                    vector = uo_ref[c, plane, :, lanes]
                    if plane in ENDS:
                        vector = fo_ref[c, ENDS.index(plane), :, lanes]
                    product = vector * ko_ref[c, plane, :, lanes]
                    energy = energy + product[:NODES] + product[NODES:]
        for place, elem in enumerate(elems):
            sub = slice(place * NODES, (place + 1) * NODES)
            scale = elem_ref[elem * NODES : (elem + 1) * NODES, lanes]
            zout = [[zout_ref[c, end, sub, lanes] for end in range(2)] for c in range(5)]
            kept = [[keep_ref[c, end, sub, lanes] for end in range(2)] for c in range(8)]
            back = (
                [kept[3][end] + zout[0][end] for end in range(2)],
                kept[4],
                zout[1],
            )
            for c in range(3):
                factor = scale * (DIAG if c == 0 else SHEAR)
                pairs = (
                    ([factor * add_ref[c, end, sub, lanes] for end in range(2)], THROUGH, 1),
                    (kept[c], ONWARD, -1),
                    (back[c], BACKWARD, -1),
                )
                pairs = [(v[0] + v[1], v[0] - v[1], table, sign) for v, table, sign in pairs]
                for i in range(HALF):
                    plus = minus = None
                    for even, odd, table, sign in pairs:
                        plus, minus = spread_pair(plus, minus, table, i, sign, even, odd)
                    for plane, value in ((i, plus + minus), (ORDER - i, plus - minus)):
                        value = value + kin_ref[c, plane, sub, lanes]
                        if plane in ENDS:
                            end = ENDS.index(plane)
                            value = value + (kept[5 + c][end] + zout[2 + c][end])
                            vector = None if outer else face_ref[c, end, sub, lanes]
                        elif not outer:
                            vector = u_ref[c, plane, sub, lanes]
                        k_ref[c, plane, sub, lanes] = value
                        if not outer:
                            energy = energy + value * vector
        return energy

    energy = jnp.zeros((NODES, LANES), jnp.float32)
    for tile in range(n_tile):
        energy = tile_energy(tile, energy)
    if outer:
        put_rows(
            lambda comp, plane: k_ref[comp, plane, 0:1, :],
            lambda comp, plane: k_ref[comp, plane, size_y - 1 : size_y, :],
            near_ref,
            far_ref,
        )
        return
    square = squares_refs[0][...] + squares_refs[1][...]
    for group, ref in ((elems, face_ref), ((0, n_elem - 1), fo_ref)):
        for place, elem in enumerate(group):
            own = slice(place * NODES, (place + 1) * NODES)
            rows = slice(elem * NODES, (elem + 1) * NODES)
            for end, plane in enumerate(ENDS):
                part = None
                for comp in range(comps):
                    strip = ref[comp, end, own, :]
                    part = strip * strip if part is None else part + strip * strip
                square = square + fold(part * halfz_ref[0:1, :]) * half_ref[plane, rows, :]
    moments = [carry_ref[i] for i in range(4)]
    moments[2 * slot] = moments[2 * slot] + square
    moments[2 * slot + 1] = moments[2 * slot + 1] + energy
    if not last:
        for i in range(4):
            sums_ref[i] = moments[i]
    else:
        lane = lax.broadcasted_iota(jnp.int32, sums_ref.shape, 1)
        known = jnp.zeros(sums_ref.shape, jnp.float32)
        for i in range(4):
            known = jnp.where(lane == i, jnp.sum(moments[i]), known)
        sums_ref[...] = known


def put_rows(lo_of, hi_of, near_ref, far_ref):
    y_upper = is_upper("gy")
    comps, planes, _ = near_ref.shape
    for comp in range(comps):
        for plane in range(planes):
            row = slice(plane, plane + 1)
            far_ref[comp, row, :], near_ref[comp, row, :] = pick(
                y_upper, hi_of(comp, plane), lo_of(comp, plane)
            )


def scale_kernel(flags_ref, widen_ref, weight_ref, scale_ref):
    solid = (flags_ref[...] == 1).astype(jnp.bfloat16)
    solid = jnp.dot(solid, widen_ref[...], preferred_element_type=jnp.float32)
    modulus = jnp.where(solid > 0.5, SOLID_MODULUS, VOID_MODULUS).astype(jnp.float32)
    for elem in range(flags_ref.shape[0]):
        scale_ref[elem * NODES : (elem + 1) * NODES, :] = (
            modulus[elem : elem + 1, :] * weight_ref[...]
        )


def rows_kernel(v_ref, near_ref, far_ref):
    size_y = v_ref.shape[2]
    put_rows(
        lambda comp, plane: v_ref[comp, plane, 0:1, :],
        lambda comp, plane: v_ref[comp, plane, size_y - 1 : size_y, :],
        near_ref,
        far_ref,
    )


def side_rows(comp, elem, n_elem):
    start = comp * (n_elem * ORDER + 1) + elem * ORDER
    return slice(start, start + NODES)


def faces_kernel(*refs, n_elem):
    vmid_ref, vedge_ref, ynear_ref, yfar_ref = refs[:4]
    near_ref, far_ref = refs[-2:]
    comps = vmid_ref.shape[0]
    x_upper, y_upper = is_upper("gx"), is_upper("gy")
    v_refs = vmid_ref, vedge_ref
    for comp in range(comps):
        sides = [y_sides(y_upper, ynear_ref, yfar_ref, comp, plane) for plane in ENDS]
        for elem in range(n_elem):
            rows = side_rows(comp, elem, n_elem)
            lo, hi = [
                row_sum_y(v_refs, *side, comp, plane, elem, n_elem)
                for plane, side in zip(ENDS, sides)
            ]
            near_ref[rows, :], far_ref[rows, :] = pick(x_upper, lo, hi)


def assemble_kernel(kmid_ref, kedge_ref, free_ref, w_ref, done_ref, *, elems, n_elem):
    for place, elem in enumerate(elems):
        own = slice(place * NODES, (place + 1) * NODES)
        sub = slice(elem * NODES, (elem + 1) * NODES)
        for plane in range(w_ref.shape[1]):
            for comp in range(w_ref.shape[0]):
                rows = row_sum_y((kmid_ref, kedge_ref), None, None, comp, plane, elem, n_elem)
                w_ref[comp, plane, own, :] = release(sum_z(rows), free_ref[plane, sub, :])
    done_ref[...] = w_ref[0, 0, 0:NODES, :LANES]


def finish_kernel(*refs):
    *k_refs, w_ref = refs[:3]
    ynear_ref, yfar_ref, xnear_ref, xfar_ref, free_ref = refs[3:8]
    r_refs, r_faces, q_refs, q_faces = refs[8:10], refs[10:12], refs[12:14], refs[14:16]
    sums_ref, adj_out, res_out, adj_ref, res_ref, sem_ref = refs[16:]
    planes, comps, size_y, _ = adj_ref.shape
    n_elem = size_y // NODES
    x_upper, y_upper = is_upper("gx"), is_upper("gy")
    sums = jnp.sum(sums_ref[...], axis=0, keepdims=True)
    lane = lax.broadcasted_iota(jnp.int32, sums.shape, 1)
    m0, m1, m2, m3 = [
        jnp.sum(jnp.where(lane == i, sums, 0.0), axis=1, keepdims=True) for i in range(4)
    ]
    first = m0 / m1
    following = first * first * m2 - m0
    ratio = following / m0
    grow = 1.0 + ratio
    second = following / (grow * grow * m1 - 2.0 * first * grow * m2 + first * first * m3)
    lead = first + second * grow
    cross = first * second
    copies = []
    for plane in range(planes):
        end = ENDS.index(plane) if plane in ENDS else None
        place = plane if end is None else end
        for comp in range(comps):
            for elem in range(n_elem):
                sub = slice(elem * NODES, (elem + 1) * NODES)
                r_ref, row = locate(r_refs if end is None else r_faces, elem, n_elem)
                q_ref, row = locate(q_refs if end is None else q_faces, elem, n_elem)
                own = slice(row, row + NODES)
                strip = None
                if end is not None:
                    strip = x_side(x_upper, xnear_ref, xfar_ref, comp, elem, n_elem, end)
                if elem in (0, n_elem - 1):
                    lo, hi = y_sides(y_upper, ynear_ref, yfar_ref, comp, plane)
                    rows = row_sum_y(k_refs, lo, hi, comp, plane, elem, n_elem)
                    strip = rows if strip is None else strip + rows
                if strip is not None:
                    strip = release(sum_z(strip), free_ref[plane, sub, :])
                if elem not in (0, n_elem - 1):
                    rows = w_ref[comp, plane, own, :]
                    strip = rows if strip is None else strip + rows
                loads = r_ref[comp, place, own, :]
                image = q_ref[comp, place, own, :]
                adj_ref[plane, comp, sub, :] = lead * loads - cross * image
                res_ref[plane, comp, sub, :] = loads - lead * image + cross * strip
        for which, (ref, out) in enumerate(((adj_ref, adj_out), (res_ref, res_out))):
            copy = pltpu.make_async_copy(ref.at[plane], out.at[:, plane], sem_ref.at[which, plane])
            copy.start()
            copies.append(copy)
    for copy in copies:
        copy.wait()


def swap(near_out, far_out, axis):
    count = lax.axis_size(axis)
    inner = [(i, i ^ 1) for i in range(count)]
    outer = [(i, ((i + 1) ^ 1) - 1) for i in range(1, count - 1)]
    far = lax.ppermute(far_out, axis, outer)
    near = lax.ppermute(near_out, axis, inner)
    return near, far


def local(rhs_loads, flags, fixed):
    comps, size_x, size_y, size_z = rhs_loads.shape
    axes = ("gx", "gy")
    devices = lax.axis_size("gx") * lax.axis_size("gy")
    f32 = jnp.float32
    y_side = jax.ShapeDtypeStruct((comps, size_x, size_z), f32)
    side_len = comps * (size_y // NODES * ORDER + 1)
    side = jax.ShapeDtypeStruct((side_len + -side_len % NODES, size_z), f32)
    whole = pl.BlockSpec(memory_space=pltpu.VMEM)

    n_elem, n_deep = flags.shape[1:]
    widen = jnp.asarray(np.kron(np.eye(n_deep), np.ones((1, NODES))), jnp.bfloat16)
    weight_yz = jnp.asarray(WEIGHTS[:, None] * np.tile(WEIGHTS, n_deep)[None, :], f32)
    elem_scale = pl.pallas_call(
        scale_kernel,
        in_specs=[whole] * 3,
        out_specs=whole,
        out_shape=jax.ShapeDtypeStruct((size_y, size_z), f32),
        compiler_params=pltpu.CompilerParams(vmem_limit_bytes=VMEM_LIMIT),
        cost_estimate=pl.CostEstimate(flops=1000, bytes_accessed=100000, transcendentals=0),
        name="scale",
    )(flags[0], widen, weight_yz)
    free = 1.0 - fixed.astype(f32)[:, :, None] * (jnp.arange(LANES) == 0).astype(f32)
    half_xy = (
        shared_halves(size_x, lax.axis_index("gx") * size_x, size_x * lax.axis_size("gx"), NODES)[
            :, None, None
        ]
        * shared_halves(
            size_y, lax.axis_index("gy") * size_y, size_y * lax.axis_size("gy"), NODES
        )[None, :, None]
        * jnp.ones((LANES,), f32)
    )
    half_z = jnp.broadcast_to(shared_halves(size_z, 0, size_z, NODES)[None], (NODES, size_z))
    z_mat = jnp.asarray(np.stack([z_table(DERIV.T), z_table(DERIV)]))
    y_col = jnp.asarray(
        np.broadcast_to(
            np.stack([DERIV.T, DERIV])[:, :, :, None], (2, NODES, NODES, LANES)
        ),
        f32,
    )

    mid, edge = parts(n_elem)
    tables = (free, elem_scale, half_xy, half_z, z_mat, y_col)

    def shape(*sizes):
        return jax.ShapeDtypeStruct(sizes, f32)

    def call(
        kernel, name, args, out_shape, scratch=(), us=1.0, out_spec=whole
    ):
        return pl.pallas_call(
            kernel,
            in_specs=[whole] * len(args),
            out_specs=[out_spec] * len(out_shape),
            out_shape=list(out_shape),
            scratch_shapes=list(scratch),
            compiler_params=pltpu.CompilerParams(vmem_limit_bytes=VMEM_LIMIT),
            cost_estimate=pl.CostEstimate(
                flops=int(us * 4e6), bytes_accessed=int(us * 2.5e6), transcendentals=0
            ),
            name=name,
        )(*args)

    def main(v, y_halo, elems, name):
        some = (comps, size_x, len(elems) * NODES, size_z)
        return call(
            functools.partial(main_kernel, elems=elems, n_elem=n_elem),
            name,
            (*v, *y_halo, *tables),
            (shape(*some), shape(*some), shape(NODES, LANES)),
            (
                pltpu.VMEM(some, f32),
                pltpu.VMEM(some, f32),
                pltpu.VMEM((comps, size_x, NODES, LANES), f32),
                pltpu.VMEM((comps, size_x, NODES, LANES), f32),
            ),
            us=5.0,
        )

    def update(u, k, x_halo, squares, others, elems, slot, name):
        rows = len(elems) * NODES
        last = slot == 1 and 0 not in elems
        out = [shape(comps, size_x, rows, size_z), shape(comps, 2, rows, size_z)]
        if 0 in elems:
            out += [y_side, y_side]
        else:
            out += [shape(devices, LANES) if last else shape(4, NODES, LANES)]
        return call(
            functools.partial(update_kernel, elems=elems, n_elem=n_elem, slot=slot, last=last),
            name,
            (u, k, *x_halo, *tables, *squares, *others),
            out,
            (
                pltpu.VMEM((comps, 2, rows, size_z), f32),
                pltpu.VMEM((comps, 2, rows, size_z), f32),
                pltpu.VMEM((8, 2, rows, size_z), f32),
                pltpu.VMEM((5, 2, rows, size_z), f32),
                pltpu.VMEM((5, 2, rows, size_z), f32),
                pltpu.VMEM((5, 2, NODES, LANES), f32),
            ),
            us=2.0,
        )

    def y_halos(y_rows):
        return swap(*y_rows, "gy")

    def x_halos(v, y_halo, after):
        sides = call(
            functools.partial(faces_kernel, n_elem=n_elem),
            "faces",
            (*v, *y_halo, *after),
            (side, side),
            us=0.3,
        )
        return swap(*sides, "gx")

    def step(v, y_rows, carry, slot):
        y_halo = y_halos(y_rows)
        u_mid, k_mid, sq_mid = main(v, (), mid, "middle")
        x_halo = x_halos(v, y_halo, ())
        u_edge, k_edge, sq_edge = main(v, y_halo, edge, "edges")
        squares = sq_mid, sq_edge
        k_edge, f_edge, *y_rows = update(
            u_edge, k_edge, x_halo, squares, (), edge, slot, "update_edges"
        )
        outer = u_edge, k_edge, f_edge, carry
        k_mid, f_mid, carry = update(
            u_mid, k_mid, x_halo, squares, outer, mid, slot, "update_middle"
        )
        return (k_mid, k_edge), (u_mid, u_edge, f_mid, f_edge), y_rows, carry

    y_rows = call(rows_kernel, "rows", (rhs_loads,), (y_side, y_side), us=0.1)
    carry = jnp.zeros((4, NODES, LANES), f32)
    k_loads, loads, y_rows, carry = step((rhs_loads, rhs_loads), y_rows, carry, 0)
    k_image, image, y_rows, sums = step(k_loads, y_rows, carry, 1)
    y_halo = y_halos(y_rows)
    w_mid, done = call(
        functools.partial(assemble_kernel, elems=mid, n_elem=n_elem),
        "assemble",
        (*k_image, free),
        (shape(comps, size_x, len(mid) * NODES, size_z), shape(NODES, LANES)),
        us=1.0,
    )
    x_halo = x_halos(k_image, y_halo, (done,))
    sums = lax.all_to_all(sums, axes, 0, 0, tiled=True)
    return tuple(
        call(
            finish_kernel,
            "finish",
            (*k_image, w_mid, *y_halo, *x_halo, free, *loads, *image, sums),
            (shape(*rhs_loads.shape),) * 2,
            (
                pltpu.VMEM((size_x, comps, size_y, size_z), f32),
                pltpu.VMEM((size_x, comps, size_y, size_z), f32),
                pltpu.SemaphoreType.DMA((2, size_x)),
            ),
            us=4.0,
            out_spec=pl.BlockSpec(memory_space=pltpu.HBM),
        )
    )


def solution(mesh):
    in_specs = (P(None, "gx", "gy", None), P("gx", "gy", None), P("gx", "gy"))
    out_specs = (P(None, "gx", "gy", None), P(None, "gx", "gy", None))
    return jax.shard_map(local, mesh=mesh, in_specs=in_specs, out_specs=out_specs, check_vma=False)
```
